32 devices in a mesh: groups: 2 (over y), expert: 4 (over z), blk: 2 (over x), tensor: 2 (over core).
Axes of the slice: x: 2, y: 2, z: 4, core: 2. Of those that a mesh axis runs over, the one named last changes fastest.
Arguments:
- tokens: bfloat16 [2048, 1024], P(('groups', 'expert', 'blk')), parts along dimension 0, may hold values from -6 to 6
- cotangent: bfloat16 [2048, 1024], P(('groups', 'expert', 'blk')), parts along dimension 0, may hold values from -6 to 6
- probs: bfloat16 [2048, 6], P(('groups', 'expert', 'blk')), parts along dimension 0, may hold values from 0.049804688 to 0.59765625
- experts: int32 [2048, 6], P(('groups', 'expert', 'blk')), parts along dimension 0, may hold values from 0 to 63, all different within a row; in each aligned block of 128 rows (0 to 127, 128 to 255, ...) at most 16 rows name the same one
- w_gate: bfloat16 [128, 1024, 352], P(('expert', 'blk'), None, 'tensor'), may hold values from -0.1875 to 0.1875
- w_up: bfloat16 [128, 1024, 352], P(('expert', 'blk'), None, 'tensor'), may hold values from -0.1875 to 0.1875
- w_down: bfloat16 [128, 352, 1024], P(('expert', 'blk'), 'tensor'), may hold values from -0.21875 to 0.21875
Outputs:
- grad_tokens: bfloat16 [2048, 1024], P(('groups', 'expert', 'blk')), parts along dimension 0
- grad_probs: float32 [2048, 6], P(('groups', 'expert', 'blk')), parts along dimension 0
- grad_gate: bfloat16 [256, 1024, 352], P(('groups', 'expert', 'blk'), None, 'tensor'), parts along dimension 0
- grad_up: bfloat16 [256, 1024, 352], P(('groups', 'expert', 'blk'), None, 'tensor'), parts along dimension 0
- grad_down: bfloat16 [256, 352, 1024], P(('groups', 'expert', 'blk'), 'tensor'), parts along dimension 0
The draws below stay inside these ranges and needn't reach their ends.
There are 2 independent parts, one for each index of `groups`. The reference program is written for one: setup_inputs(seed, part) draws one part's arguments, and reference() takes and returns one part's arrays. A program takes and returns all parts, laid end to end along the dimension named above; an argument that names none is the same for every part. Nothing has to cross between parts.
Inputs may be any that keep to these rules, and one draw needn't show every extreme that they name: Each row names 6 different experts. Within the rows of one device no expert is named more than 16 times; in every draw some expert is named exactly 16 times by one device's rows.
All inputs are finite; a program needn't handle non-finite values.
Results may differ from the reference program's by a relative error of at most 0.0065.
Values may be sent and summed in bfloat16 or wider, within the bound.
No kernel may reach another device: no remote copies, remote signals or barrier semaphores. Data moves between devices by JAX's collectives and lax.ppermute only.
A program may use at most 192 MiB of HBM per device.

```python
import math
import jax
import jax.numpy as jnp
import numpy as np
from jax import lax

D = 1024
FF = 704
EXPERTS = 64
TOP = 6
TOK_DEV = 128
MOST = 16
HALVES = 128
TOKENS = 1024


def levels(stream_key, shape, split, least, top_value):
    loudness = 1.0
    for dim, blocks in split:
        steps = jax.random.uniform(jax.random.fold_in(jax.random.fold_in(stream_key, 6), dim), (blocks,), jnp.float32, least / len(split), top_value / len(split))
        loudness = loudness * jnp.repeat(jnp.exp(steps), shape[dim] // blocks).reshape((-1,) + (1,) * (len(shape) - 1 - dim))
    return loudness


def routed_block(rng, own, number, rows, amount, top, most, slope):
    sequence = jax.random.permutation(rng, amount)
    heavy_load, ordinary = portions_of(amount, rows * top, most, slope, True), portions_of(amount, rows * top, most, slope, False)
    places = jnp.arange(amount)

    def named(lengths, offset_by):
        used = int((lengths > 0).sum())
        fixed = max(1, used // 4)
        shifted = fixed + (places - fixed + offset_by * (used - fixed)) % max(1, amount - fixed)
        return jnp.zeros((amount,), jnp.int32).at[sequence[jnp.where(places < fixed, places, shifted)]].set(jnp.asarray(lengths, jnp.int32))

    lengths = jnp.where(number % 4 == 0, named(heavy_load, number // 4), named(ordinary, number - number // 4 - 1))
    mixed = jax.random.permutation(jax.random.fold_in(own, 3), amount)
    donor, receiver = mixed[0:amount // 2 * 2:2], mixed[1:amount // 2 * 2:2]
    room = jnp.minimum(lengths[donor] - 1, most - lengths[receiver]) // 2
    room = jnp.where((donor == sequence[0]) | (receiver == sequence[0]) | (lengths[receiver] == 0), 0, jnp.maximum(room, 0))
    shifted = jax.random.randint(jax.random.fold_in(own, 4), (amount // 2,), 0, 1 << 20) % (room + 1)
    lengths = lengths.at[donor].add(-shifted).at[receiver].add(shifted)
    labels = jnp.searchsorted(jnp.cumsum(lengths), jnp.arange(rows * top), side="right").astype(jnp.int32)
    listing = labels.reshape(top, rows).T
    listing = listing[jax.random.permutation(jax.random.fold_in(own, 1), rows)]
    offset_by = jax.random.randint(jax.random.fold_in(own, 2), (rows, 1), 0, top)
    return jnp.take_along_axis(listing, (jnp.arange(top)[None, :] + offset_by) % top, axis=1)


def portions_of(amount, total, limit, slope, full):
    loads = [(1 << 20) // math.isqrt(grade ** slope) + 1 for grade in range(1, amount + 1)]
    largest = limit if full else min(limit, max(-(-total // amount), total * loads[0] // sum(loads)))
    least = 1 if total - largest >= amount - 1 else 0
    given, surplus = [largest] + [least] * (amount - 1), total - largest - least * (amount - 1)
    while surplus > 0:
        movable = [i for i in range(1, amount) if given[i] < largest] or [i for i in range(1, amount) if given[i] < limit]
        mass, budget = sum([loads[i] for i in movable]), surplus
        for i in movable:
            extra = min(limit - given[i], max(1, budget * loads[i] // mass), surplus)
            given[i] = given[i] + extra
            surplus = surplus - extra
    return np.array(given)


def scatter_about(stream_key, shape, spread, most, shards=(), kind=jnp.bfloat16):
    drawn = spread * jax.random.normal(stream_key, shape, jnp.float32)
    if shards:
        drawn = drawn * levels(stream_key, shape, shards, -0.22, 0.18)
    return jnp.clip(drawn, -most, most).astype(kind)


def setup_inputs(seed: int = 0, part: int = 0) -> dict:
    splits = jax.random.split(jax.random.key(seed), 8)
    part_splits = jax.random.split(jax.random.fold_in(splits[7], part), 8)
    tokens = scatter_about(part_splits[0], (TOKENS, D), 1.0, 6.0, ((0, 8),))
    cotangent = scatter_about(part_splits[1], (TOKENS, D), 1.0, 6.0, ((0, 8),))
    probs = jnp.clip(0.049804688 + 0.54785156 * jax.random.uniform(part_splits[2], (TOKENS, TOP), jnp.float32) ** levels(part_splits[2], (TOKENS, TOP), ((0, 8),), -0.2, 0.2), 0.049804688, 0.59765625).astype(jnp.bfloat16)
    experts_keys = jax.random.split(jax.random.fold_in(part_splits[3], 1), TOKENS // TOK_DEV)
    experts_turns = jax.random.permutation(jax.random.fold_in(part_splits[3], 3), TOKENS // TOK_DEV)
    experts = jax.vmap(lambda own, number: routed_block(jax.random.fold_in(part_splits[3], 2), own, number, TOK_DEV, EXPERTS, TOP, MOST, 2))(experts_keys, experts_turns).reshape((TOKENS, TOP))
    w_gate = scatter_about(splits[4], (HALVES, D, FF // 2), D ** -0.5, 0.1875, ((0, 8), (2, 2)))
    w_up = scatter_about(splits[5], (HALVES, D, FF // 2), D ** -0.5, 0.1875, ((0, 8), (2, 2)))
    w_down = scatter_about(splits[6], (HALVES, FF // 2, D), FF ** -0.5, 0.21875, ((0, 8), (1, 2)))
    return {"tokens": tokens, "cotangent": cotangent, "probs": probs, "experts": experts, "w_gate": w_gate, "w_up": w_up, "w_down": w_down}


def quarter_pass(rows_x, rows_dy, rows_prob, gate_part, up_part, down_part):
    gate_value = jnp.dot(rows_x, gate_part, preferred_element_type=jnp.float32)
    up_value = jnp.dot(rows_x, up_part, preferred_element_type=jnp.float32)
    sigmoid_value = jax.nn.sigmoid(gate_value)
    active = gate_value * sigmoid_value
    hidden = active * up_value
    gate_scale = rows_prob.astype(jnp.float32)[:, None]
    gated_hidden = (gate_scale * hidden).astype(jnp.bfloat16)
    raw_grad = jnp.dot(rows_dy, down_part.T, preferred_element_type=jnp.float32)
    prob_part = jnp.sum(hidden * raw_grad, axis=1).astype(jnp.bfloat16)
    grad_hidden = gate_scale * raw_grad
    grad_gate = (grad_hidden * up_value * sigmoid_value * (1.0 + gate_value * (1.0 - sigmoid_value))).astype(jnp.bfloat16)
    grad_up = (grad_hidden * active).astype(jnp.bfloat16)
    weight_gate = jnp.dot(rows_x.T, grad_gate, preferred_element_type=jnp.float32)
    weight_up = jnp.dot(rows_x.T, grad_up, preferred_element_type=jnp.float32)
    weight_down = jnp.dot(gated_hidden.T, rows_dy, preferred_element_type=jnp.float32)
    input_part = (jnp.dot(grad_gate, gate_part.T, preferred_element_type=jnp.float32)
                  + jnp.dot(grad_up, up_part.T, preferred_element_type=jnp.float32)).astype(jnp.bfloat16)
    return input_part, prob_part, weight_gate, weight_up, weight_down


def reference(tokens, cotangent, probs, experts, w_gate, w_up, w_down):
    token_count, features = tokens.shape
    top_count = experts.shape[1]
    flat_experts = experts.reshape(-1).astype(jnp.int32)
    assign_total = flat_experts.shape[0]
    span_rows = MOST * (token_count // TOK_DEV)
    sorted_ids = jnp.argsort(flat_experts, stable=True).astype(jnp.int32)
    expert_ids = jnp.arange(EXPERTS, dtype=jnp.int32)
    counts = jnp.sum((flat_experts[:, None] == expert_ids[None, :]).astype(jnp.int32), axis=0)
    starts = (jnp.cumsum(counts) - counts).astype(jnp.int32)
    padded_ids = jnp.concatenate([sorted_ids, jnp.full((span_rows,), assign_total, jnp.int32)])
    padded_x = jnp.concatenate([tokens, jnp.zeros((1, features), tokens.dtype)])
    padded_dy = jnp.concatenate([cotangent, jnp.zeros((1, features), cotangent.dtype)])
    padded_prob = jnp.concatenate([probs.reshape(-1), jnp.zeros((1,), probs.dtype)])
    quarter = w_gate.shape[2] // 2

    def per_expert(carry, expert_index):
        input_acc, prob_acc = carry
        chosen = lax.dynamic_slice_in_dim(padded_ids, starts[expert_index], span_rows)
        filled = jnp.arange(span_rows, dtype=jnp.int32) < counts[expert_index]
        chosen = jnp.where(filled, chosen, assign_total).astype(jnp.int32)
        token_ids = (chosen // top_count).astype(jnp.int32)
        rows_x = padded_x[token_ids]
        rows_dy = padded_dy[token_ids]
        rows_prob = padded_prob[chosen]
        gate_pair = lax.dynamic_slice_in_dim(w_gate, (2 * expert_index).astype(jnp.int32), 2, 0)
        up_pair = lax.dynamic_slice_in_dim(w_up, (2 * expert_index).astype(jnp.int32), 2, 0)
        down_pair = lax.dynamic_slice_in_dim(w_down, (2 * expert_index).astype(jnp.int32), 2, 0)
        results = {}
        for half_index in range(2):
            for tensor_index in range(2):
                lower = tensor_index * quarter
                results[(half_index, tensor_index)] = quarter_pass(
                    rows_x, rows_dy, rows_prob,
                    gate_pair[half_index][:, lower:lower + quarter],
                    up_pair[half_index][:, lower:lower + quarter],
                    down_pair[half_index][lower:lower + quarter, :])
        input_total = jnp.zeros((span_rows, features), jnp.float32)
        prob_total = jnp.zeros((span_rows,), jnp.float32)
        for tensor_index in range(2):
            first_part = results[(0, tensor_index)]
            second_part = results[(1, tensor_index)]
            pair_input = (first_part[0].astype(jnp.float32) + second_part[0].astype(jnp.float32)).astype(jnp.bfloat16)
            pair_prob = (first_part[1].astype(jnp.float32) + second_part[1].astype(jnp.float32)).astype(jnp.bfloat16)
            input_total = input_total + lax.optimization_barrier(pair_input).astype(jnp.float32)
            prob_total = prob_total + lax.optimization_barrier(pair_prob).astype(jnp.float32)
        input_acc = input_acc.at[token_ids].add(input_total)
        prob_acc = prob_acc.at[chosen].add(prob_total)
        gate_grad = jnp.stack([jnp.concatenate([results[(half_index, 0)][2], results[(half_index, 1)][2]], axis=1)
                               for half_index in range(2)]).astype(jnp.bfloat16)
        up_grad = jnp.stack([jnp.concatenate([results[(half_index, 0)][3], results[(half_index, 1)][3]], axis=1)
                             for half_index in range(2)]).astype(jnp.bfloat16)
        down_grad = jnp.stack([jnp.concatenate([results[(half_index, 0)][4], results[(half_index, 1)][4]], axis=0)
                               for half_index in range(2)]).astype(jnp.bfloat16)
        return (input_acc, prob_acc), (gate_grad, up_grad, down_grad)

    initial = (jnp.zeros((token_count + 1, features), jnp.float32), jnp.zeros((assign_total + 1,), jnp.float32))
    (input_acc, prob_acc), (gate_grads, up_grads, down_grads) = lax.scan(per_expert, initial, expert_ids)
    grad_tokens = input_acc[:token_count].astype(jnp.bfloat16)
    grad_probs = prob_acc[:assign_total].reshape(token_count, top_count)
    grad_gate = gate_grads.reshape(w_gate.shape)
    grad_up = up_grads.reshape(w_up.shape)
    grad_down = down_grads.reshape(w_down.shape)
    return grad_tokens, grad_probs, grad_gate, grad_up, grad_down
```

```python
import functools

import jax
import jax.numpy as jnp
from jax import lax
from jax.experimental import pallas as pl
from jax.experimental.pallas import tpu as pltpu
from jax.sharding import PartitionSpec as P

MOST = 16
BF16, F32 = jnp.bfloat16, jnp.float32
LAST = (((1,), (1,)), ((), ()))
LEAD = (((0,), (0,)), ((), ()))
VMEM_BYTES = 56 * 1024 * 1024


def dot(a, b, dims):
    return lax.dot_general(a, b, dims, preferred_element_type=F32)


def iota(shape, dim):
    return lax.broadcasted_iota(jnp.int32, shape, dim)


def ranks_and_probs(first, meta, span, count):
    sources, height, tokens = meta.shape
    kinds = height // 2
    wanted = ((first + span * iota((count, tokens), 0)) >> 1).astype(F32)
    named, weight = [], []
    for source in range(sources):
        entry = meta[source].astype(F32)
        hit = jnp.zeros((count, tokens), F32)
        prob = jnp.zeros((count, tokens), F32)
        for kind in range(kinds):
            same = entry[kind : kind + 1] == wanted
            hit = jnp.where(same, 1.0, hit)
            prob = jnp.where(same, entry[kinds + kind : kinds + kind + 1], prob)
        named.append(hit)
        weight.append(prob)
    named = jnp.concatenate(named)
    before = (iota((tokens, tokens), 0) < iota((tokens, tokens), 1)).astype(F32).astype(BF16)
    rank = jnp.dot(named.astype(BF16), before, preferred_element_type=F32)
    return jnp.where(named > 0, rank, -1.0), jnp.concatenate(weight)


def slot_matrix(rank):
    count, tokens = rank.shape
    wide = jnp.broadcast_to(rank[:, None, :], (count, MOST, tokens)).reshape(count * MOST, tokens)
    place = (iota((count * MOST, tokens), 0) & (MOST - 1)).astype(F32)
    return jnp.where(wide == place, 1.0, 0.0).astype(BF16)


def gather_rows(step, rank, pieces, rows_scr):
    count = rows_scr.shape[0]
    near, far = pieces
    half = near.shape[1]
    sources = near.shape[0]
    for source in range(sources):
        pick = slot_matrix(rank[source * count : (source + 1) * count])
        both = jnp.concatenate([near[source], far[source]], axis=0)
        rows = jnp.dot(pick, both, preferred_element_type=F32).astype(BF16)
        start = pl.multiple_of((step * sources + source) * MOST, MOST)
        rows_scr[:, pl.ds(start, MOST), :] = rows.reshape(count, MOST, rows.shape[1])
    del half


def first_kernel(steps, span, first_ref, meta_ref, near_ref, far_ref, wg_ref, wu_ref, rows_ref, gate_ref, up_ref,
                 rows_scr):
    step = pl.program_id(0)
    count = rows_scr.shape[0]

    @pl.when(step < steps)
    def _():
        rank, _ = ranks_and_probs(first_ref[0], meta_ref[...], span, count)
        gather_rows(step, rank, (near_ref, far_ref), rows_scr)

    @pl.when(step >= steps)
    def _():
        rows = rows_scr[step - steps]
        rows_ref[0] = rows
        gate_ref[0] = dot(wg_ref[0], rows, LAST)
        up_ref[0] = dot(wu_ref[0], rows, LAST)


def second_kernel(steps, span, first_ref, meta_ref, near_ref, far_ref, wg_ref, wu_ref, wd_ref, gate_ref, up_ref,
                  rows_ref, dgate_ref, dup_ref, gated_ref, prob_ref, own_ref, other_ref,
                  rows_scr, rank_scr, weight_scr, input_scr):
    step = pl.program_id(0)
    count, slots, features = rows_scr.shape
    sources = near_ref.shape[0]
    all_sources = slots // MOST
    tokens = rank_scr.shape[1]
    span_rows = sources * count

    @pl.when(step < steps)
    def _():
        rank, weight = ranks_and_probs(first_ref[0], meta_ref[...], span, count)
        start = step * span_rows
        if span_rows % 8 == 0:
            start = pl.multiple_of(start, 8)
        rank_scr[pl.ds(start, span_rows)] = rank
        weight_scr[pl.ds(start, span_rows)] = weight
        gather_rows(step, rank, (near_ref, far_ref), rows_scr)

    @pl.when((step >= steps) & (step < steps + count))
    def _():
        expert = step - steps
        total = all_sources * count
        row, lane = iota((total, slots), 0), iota((total, slots), 1)
        spread = jnp.where(row == (lane // MOST) * count + expert, 1.0, 0.0).astype(BF16)
        place = (iota((tokens, slots), 1) & (MOST - 1)).astype(F32)
        holds = dot(rank_scr[...].astype(BF16), spread, LEAD) == place
        weight = dot(weight_scr[...].astype(BF16), spread, LEAD)
        scale = jnp.sum(jnp.where(holds, weight, 0.0), axis=0, keepdims=True)
        rows = rows_scr[expert]
        rows_ref[0] = rows
        raw = dot(wd_ref[0], rows, LAST)
        gate, up = gate_ref[0], up_ref[0]
        sigmoid = 1.0 / (1.0 + jnp.exp(-gate))
        active = gate * sigmoid
        hidden = active * up
        gated_ref[0] = (scale * hidden).astype(BF16)
        prob = jnp.sum(hidden * raw, axis=0, keepdims=True)
        scaled = scale * raw
        dgate = (scaled * up * sigmoid * (1.0 + gate * (1.0 - sigmoid))).astype(BF16)
        dup = (scaled * active).astype(BF16)
        dgate_ref[0] = dgate
        dup_ref[0] = dup
        input_scr[expert] = (dot(dgate, wg_ref[0], LEAD) + dot(dup, wu_ref[0], LEAD)).astype(BF16)
        block = jnp.where(
            iota((all_sources, slots), 0) == iota((all_sources, slots), 1) // MOST, 1.0, 0.0
        ).astype(BF16)
        prob_ref[0] = dot(block, jnp.where(holds, prob, 0.0).astype(BF16), LAST)

    @pl.when(step >= steps + count)
    def _():
        chunk = step - steps - count
        half = own_ref.shape[1]
        for source in range(sources):
            number = chunk * sources + source
            start = number * count
            if count % 8 == 0:
                start = pl.multiple_of(start, 8)
            pick = slot_matrix(rank_scr[pl.ds(start, count)])
            rows = input_scr[:, pl.ds(pl.multiple_of(number * MOST, MOST), MOST), :].reshape(count * MOST, features)
            part = dot(pick, rows, LEAD).astype(BF16)
            own_ref[source] = part[:half]
            other_ref[source] = part[half:]


def third_kernel(x_ref, dy_ref, dgate_ref, dup_ref, gated_ref, gg_ref, gu_ref, gd_ref):
    x, dy = x_ref[0], dy_ref[0]
    gg_ref[0] = jnp.dot(dgate_ref[0], x, preferred_element_type=F32).astype(BF16)
    gu_ref[0] = jnp.dot(dup_ref[0], x, preferred_element_type=F32).astype(BF16)
    gd_ref[0] = jnp.dot(gated_ref[0], dy, preferred_element_type=F32).astype(BF16)


def shift(array, axes, sizes, by):
    pairs = []
    flat = 1
    for size in sizes:
        flat *= size
    for index in range(flat):
        rest, place = index, []
        for size in reversed(sizes):
            place.insert(0, rest % size)
            rest //= size
        to = 0
        for size, at, move in zip(sizes, place, by):
            to = to * size + (at + move) % size
        pairs.append((index, to))
    return lax.ppermute(array, axes if len(axes) > 1 else axes[0], pairs)


def per_device(tokens, cotangent, probs, experts, w_gate, w_up, w_down):
    rows, features = tokens.shape
    top = experts.shape[1]
    zs, xs = lax.axis_size("expert"), lax.axis_size("blk")
    cores = lax.axis_size("tensor")
    positions = zs * xs
    half = rows // cores
    halves, _, quarter = w_gate.shape
    span = 2 if halves % 2 == 0 else 1
    count = halves // span
    hidden = span * quarter
    slots = positions * MOST
    core = lax.axis_index("tensor")
    position = lax.axis_index("expert") * xs + lax.axis_index("blk")
    kinds = -(-top // 8) * 8

    def swap(array):
        return lax.ppermute(array, "tensor", [(i, (i + 1) % cores) for i in range(cores)])

    def own_first(array):
        return jnp.roll(array, -core * half, axis=-1)

    experts_t = own_first(experts.T)
    probs_t = own_first(probs.T)
    meta_own = jnp.concatenate(
        [
            jnp.pad(experts_t.astype(BF16), ((0, kinds - top), (0, 0)), constant_values=-1.0),
            jnp.pad(probs_t, ((0, kinds - top), (0, 0))),
        ]
    )
    order = [(d, c) for c in range(xs) for d in range(zs)]

    def to_all(array):
        return [
            array if (d, c) == (0, 0) else shift(array, ("expert", "blk"), (zs, xs), (d, c)) for d, c in order
        ]

    def gather(array):
        own = lax.dynamic_slice_in_dim(array, core * half, half, 0)
        line = [own] + [shift(own, ("expert",), (zs,), (d,)) for d in range(1, zs)]
        blocks = list(line)
        for c in range(1, xs):
            blocks += [shift(block, ("blk",), (xs,), (c,)) for block in line]
        near = jnp.stack(blocks)
        return near, swap(near)

    meta = jnp.stack(to_all(meta_own))
    near_x, far_x = gather(tokens)
    near_dy, far_dy = gather(cotangent)

    wg = jnp.swapaxes(w_gate, 1, 2).reshape(count, hidden, features)
    wu = jnp.swapaxes(w_up, 1, 2).reshape(count, hidden, features)
    wd = w_down.reshape(count, hidden, features)
    first = (position * halves).astype(jnp.int32).reshape(1)

    per_step = min(positions, 8)
    steps = positions // per_step
    last = lambda i, n: jnp.minimum(i, n - 1)
    later = lambda i, n: jnp.clip(i - steps, 0, n - 1)
    scalar = pl.BlockSpec(memory_space=pltpu.SMEM)
    meta_spec = pl.BlockSpec((per_step, 2 * kinds, rows), lambda i: (last(i, steps), 0, 0))
    piece_spec = pl.BlockSpec((per_step, half, features), lambda i: (last(i, steps), 0, 0))
    weight_spec = pl.BlockSpec((1, hidden, features), lambda i: (later(i, count), 0, 0))
    rows_spec = pl.BlockSpec((1, slots, features), lambda i: (later(i, count), 0, 0))
    hidden_spec = pl.BlockSpec((1, hidden, slots), lambda i: (later(i, count), 0, 0))
    params = pltpu.CompilerParams(vmem_limit_bytes=VMEM_BYTES, dimension_semantics=("arbitrary",))
    flops = 2 * count * hidden * slots * features

    rows_x, gate, up = pl.pallas_call(
        functools.partial(first_kernel, steps, span),
        grid=(steps + count,),
        in_specs=[scalar, meta_spec, piece_spec, piece_spec, weight_spec, weight_spec],
        out_specs=[rows_spec, hidden_spec, hidden_spec],
        out_shape=[
            jax.ShapeDtypeStruct((count, slots, features), BF16),
            jax.ShapeDtypeStruct((count, hidden, slots), F32),
            jax.ShapeDtypeStruct((count, hidden, slots), F32),
        ],
        scratch_shapes=[pltpu.VMEM((count, slots, features), BF16)],
        compiler_params=params,
        cost_estimate=pl.CostEstimate(flops=2 * flops, bytes_accessed=20_000_000, transcendentals=0),
        name="forward",
    )(first, meta, near_x, far_x, wg, wu)

    out_piece = pl.BlockSpec((per_step, half, features), lambda i: (jnp.clip(i - steps - count, 0, steps - 1), 0, 0))
    rows_dy, dgate, dup, gated, prob, own, other = pl.pallas_call(
        functools.partial(second_kernel, steps, span),
        grid=(steps + count + steps,),
        in_specs=[scalar, meta_spec, piece_spec, piece_spec, weight_spec, weight_spec, weight_spec, hidden_spec,
                  hidden_spec],
        out_specs=[
            rows_spec, hidden_spec, hidden_spec, hidden_spec,
            pl.BlockSpec((1, positions, rows), lambda i: (later(i, count), 0, 0)),
            out_piece, out_piece,
        ],
        out_shape=[
            jax.ShapeDtypeStruct((count, slots, features), BF16),
            jax.ShapeDtypeStruct((count, hidden, slots), BF16),
            jax.ShapeDtypeStruct((count, hidden, slots), BF16),
            jax.ShapeDtypeStruct((count, hidden, slots), BF16),
            jax.ShapeDtypeStruct((count, positions, rows), F32),
            jax.ShapeDtypeStruct((positions, half, features), BF16),
            jax.ShapeDtypeStruct((positions, half, features), BF16),
        ],
        scratch_shapes=[
            pltpu.VMEM((count, slots, features), BF16),
            pltpu.VMEM((positions * count, rows), F32),
            pltpu.VMEM((positions * count, rows), F32),
            pltpu.VMEM((count, slots, features), BF16),
        ],
        compiler_params=params,
        cost_estimate=pl.CostEstimate(flops=3 * flops, bytes_accessed=30_000_000, transcendentals=0),
        name="backward",
    )(first, meta, near_dy, far_dy, wg, wu, wd, gate, up)

    w_spec = pl.BlockSpec((1, hidden, features), lambda i: (i, 0, 0))
    r_spec = pl.BlockSpec((1, slots, features), lambda i: (i, 0, 0))
    h_spec = pl.BlockSpec((1, hidden, slots), lambda i: (i, 0, 0))
    grad_gate, grad_up, grad_down = pl.pallas_call(
        third_kernel,
        grid=(count,),
        in_specs=[r_spec, r_spec, h_spec, h_spec, h_spec],
        out_specs=[w_spec] * 3,
        out_shape=[jax.ShapeDtypeStruct((count, hidden, features), BF16)] * 3,
        compiler_params=params,
        cost_estimate=pl.CostEstimate(flops=3 * flops, bytes_accessed=24_000_000, transcendentals=0),
        name="weights",
    )(rows_x, rows_dy, dgate, dup, gated)

    chip = (own.astype(F32) + swap(other).astype(F32)).astype(BF16).reshape(xs, zs, half, features)
    line = chip[0].astype(F32)
    for c in range(1, xs):
        line = line + shift(chip[c], ("blk",), (xs,), (-c,)).astype(F32)
    line = line.astype(BF16)
    total = line[0].astype(F32)
    for d in range(1, zs):
        total = total + shift(line[d], ("expert",), (zs,), (-d,)).astype(F32)
    mine = total.astype(BF16)
    theirs = swap(mine)
    grad_tokens = jnp.where(core == 0, jnp.concatenate([mine, theirs]), jnp.concatenate([theirs, mine]))

    found = jnp.zeros((top, rows), F32)
    z_at, x_at = lax.axis_index("expert"), lax.axis_index("blk")
    for number, (d, c) in enumerate(order):
        part = prob[:, number]
        if number:
            part = shift(part, ("expert", "blk"), (zs, xs), (-d, -c))
        holder = ((z_at + d) % zs) * xs + (x_at + c) % xs
        ids = (holder * halves + span * jnp.arange(count, dtype=jnp.int32)) >> 1
        found = found + jnp.sum(
            jnp.where(experts_t[:, None, :] == ids[None, :, None], part[None], 0.0), axis=1
        )
    found = jnp.roll(found, core * half, axis=-1)
    grad_probs = (found + swap(found)).T
    shape = (halves, quarter, features)
    return (
        grad_tokens,
        grad_probs,
        jnp.swapaxes(grad_gate.reshape(shape), 1, 2),
        jnp.swapaxes(grad_up.reshape(shape), 1, 2),
        grad_down.reshape(shape),
    )


def solution(mesh):
    return jax.shard_map(
        per_device,
        mesh=mesh,
        in_specs=(
            P(("groups", "expert", "blk"), None),
            P(("groups", "expert", "blk"), None),
            P(("groups", "expert", "blk"), None),
            P(("groups", "expert", "blk"), None),
            P(("expert", "blk"), None, "tensor"),
            P(("expert", "blk"), None, "tensor"),
            P(("expert", "blk"), "tensor", None),
        ),
        out_specs=(
            P(("groups", "expert", "blk"), None),
            P(("groups", "expert", "blk"), None),
            P(("groups", "expert", "blk"), None, "tensor"),
            P(("groups", "expert", "blk"), None, "tensor"),
            P(("groups", "expert", "blk"), "tensor", None),
        ),
        check_vma=False,
    )
```

```python
import functools

import jax
import jax.numpy as jnp
from jax import lax
from jax.experimental import pallas as pl
from jax.experimental.pallas import tpu as pltpu
from jax.sharding import PartitionSpec as P

MOST = 16
BF16, F32 = jnp.bfloat16, jnp.float32
LAST = (((1,), (1,)), ((), ()))
LEAD = (((0,), (0,)), ((), ()))
VMEM_BYTES = 56 * 1024 * 1024


def dot(a, b, dims):
    return lax.dot_general(a, b, dims, preferred_element_type=F32)


def iota(shape, dim):
    return lax.broadcasted_iota(jnp.int32, shape, dim)


def ranks_and_probs(first, meta, span, count):
    sources, height, tokens = meta.shape
    kinds = height // 2
    wanted = ((first + span * iota((count, tokens), 0)) >> 1).astype(F32)
    named, weight = [], []
    for source in range(sources):
        entry = meta[source].astype(F32)
        hit = jnp.zeros((count, tokens), F32)
        prob = jnp.zeros((count, tokens), F32)
        for kind in range(kinds):
            same = entry[kind : kind + 1] == wanted
            hit = jnp.where(same, 1.0, hit)
            prob = jnp.where(same, entry[kinds + kind : kinds + kind + 1], prob)
        named.append(hit)
        weight.append(prob)
    named = jnp.concatenate(named)
    before = (iota((tokens, tokens), 0) < iota((tokens, tokens), 1)).astype(F32).astype(BF16)
    rank = jnp.dot(named.astype(BF16), before, preferred_element_type=F32)
    return jnp.where(named > 0, rank, -1.0), jnp.concatenate(weight)


def slot_matrix(rank):
    count, tokens = rank.shape
    wide = jnp.broadcast_to(rank[:, None, :], (count, MOST, tokens)).reshape(count * MOST, tokens)
    place = (iota((count * MOST, tokens), 0) & (MOST - 1)).astype(F32)
    return jnp.where(wide == place, 1.0, 0.0).astype(BF16)


def gather_rows(step, rank, near, far, rows_scr):
    count, _, features = rows_scr.shape
    sources = near.shape[0]
    half = rank.shape[1] // 2
    for source in range(sources):
        pick = slot_matrix(rank[source * count : (source + 1) * count])
        both = jnp.concatenate([near[source, :half], far[source, :half]], axis=0)
        rows = jnp.dot(pick, both, preferred_element_type=F32).astype(BF16)
        start = pl.multiple_of((step * sources + source) * MOST, MOST)
        rows_scr[:, pl.ds(start, MOST), :] = rows.reshape(count, MOST, features)


def unpack_meta(near, half, tokens, kinds):
    features = near.shape[2]
    per_row = features // tokens
    lines = []
    for number in range(2 * kinds):
        at, part = half + number // per_row, number % per_row
        lines.append(near[:, at : at + 1, part * tokens : (part + 1) * tokens])
    return jnp.concatenate(lines, axis=1)


def first_kernel(steps, span, kinds, where_ref, near_ref, far_ref, wg_ref, wu_ref, rows_ref, gate_ref, up_ref,
                 rank_ref, weight_ref, meta_ref, rows_scr):
    step = pl.program_id(0)
    count = rows_scr.shape[0]
    tokens = rank_ref.shape[1]

    @pl.when(step < steps)
    def _():
        meta = unpack_meta(near_ref[:, tokens // 2 :, :].astype(F32), 0, tokens, kinds)
        rank, weight = ranks_and_probs(where_ref[0], meta, span, count)
        rank_ref[...] = rank
        meta_ref[...] = meta
        weight_ref[...] = weight
        gather_rows(step, rank, near_ref, far_ref, rows_scr)

    @pl.when(step >= steps)
    def _():
        rows = rows_scr[step - steps]
        rows_ref[0] = rows
        gate_ref[0] = dot(wg_ref[0], rows, LAST)
        up_ref[0] = dot(wu_ref[0], rows, LAST)


def second_kernel(steps, span, where_ref, rank_ref, weight_ref, meta_ref, near_ref, far_ref, wg_ref, wu_ref, wd_ref, gate_ref,
                  up_ref, rows_ref, dgate_ref, dup_ref, gated_ref, own_ref, other_ref, rows_scr, input_scr, prob_scr):
    step = pl.program_id(0)
    count, slots, features = rows_scr.shape
    sources = near_ref.shape[0]
    all_sources = slots // MOST
    tokens = rank_ref.shape[1]

    def rank_of(number, sources):
        start, size = number * count, sources * count
        if size % 8 == 0:
            start = pl.multiple_of(start, 8)
        return rank_ref[pl.ds(start, size)]

    @pl.when(step < steps)
    def _():
        gather_rows(step, rank_of(step * sources, sources), near_ref, far_ref, rows_scr)

    @pl.when((step >= steps) & (step < steps + count))
    def _():
        expert = step - steps
        total = all_sources * count
        row, lane = iota((total, slots), 0), iota((total, slots), 1)
        spread = jnp.where(row == (lane // MOST) * count + expert, 1.0, 0.0).astype(BF16)
        place = (iota((tokens, slots), 1) & (MOST - 1)).astype(F32)
        holds = dot(rank_ref[...].astype(BF16), spread, LEAD) == place
        weight = dot(weight_ref[...].astype(BF16), spread, LEAD)
        scale = jnp.sum(jnp.where(holds, weight, 0.0), axis=0, keepdims=True)
        rows = rows_scr[expert]
        rows_ref[0] = rows
        raw = dot(wd_ref[0], rows, LAST)
        gate, up = gate_ref[0], up_ref[0]
        sigmoid = 1.0 / (1.0 + jnp.exp(-gate))
        active = gate * sigmoid
        hidden = active * up
        gated_ref[0] = (scale * hidden).astype(BF16)
        prob = jnp.sum(hidden * raw, axis=0, keepdims=True)
        scaled = scale * raw
        dgate = (scaled * up * sigmoid * (1.0 + gate * (1.0 - sigmoid))).astype(BF16)
        dup = (scaled * active).astype(BF16)
        dgate_ref[0] = dgate
        dup_ref[0] = dup
        input_scr[expert] = (dot(dgate, wg_ref[0], LEAD) + dot(dup, wu_ref[0], LEAD)).astype(BF16)
        block = jnp.where(
            iota((all_sources, slots), 0) == iota((all_sources, slots), 1) // MOST, 1.0, 0.0
        ).astype(BF16)
        prob_scr[expert] = dot(block, jnp.where(holds, prob, 0.0).astype(BF16), LAST)

    @pl.when(step >= steps + count)
    def _():
        chunk = step - steps - count
        half = tokens // 2
        kinds = meta_ref.shape[1] // 2
        wanted = ((where_ref[0] + span * iota((count, tokens), 0)) >> 1).astype(F32)
        for source in range(sources):
            number = chunk * sources + source
            pick = slot_matrix(rank_of(number, 1))
            rows = input_scr[:, pl.ds(pl.multiple_of(number * MOST, MOST), MOST), :].reshape(count * MOST, features)
            part = dot(pick, rows, LEAD).astype(BF16)
            own_ref[source, :half] = part[:half]
            other_ref[source, :half] = part[half:]
            prob = prob_scr[:, pl.ds(number, 1), :].reshape(count, tokens)
            entry = meta_ref[number]
            line = [
                jnp.sum(jnp.where(entry[kind : kind + 1] == wanted, prob, 0.0), axis=0, keepdims=True)
                for kind in range(kinds)
            ]
            flip = [pltpu.roll(jnp.broadcast_to(part, (8, tokens)), half, 1)[:1] for part in line]
            tail_ref_rows = own_ref.shape[1] - half
            per_row = features // tokens
            for ref, parts in ((own_ref, line), (other_ref, flip)):
                lines = [jnp.concatenate(parts[at : at + per_row], axis=1) for at in range(0, kinds, per_row)]
                lines += [jnp.zeros_like(lines[0])] * (tail_ref_rows - len(lines))
                ref[source, half:] = jnp.concatenate(lines, axis=0).astype(BF16)


def third_kernel(x_ref, dy_ref, dgate_ref, dup_ref, gated_ref, *refs):
    gg_ref, gu_ref, gd_ref = refs[-3:]
    x, dy = x_ref[0], dy_ref[0]
    gg_ref[0] = jnp.dot(dgate_ref[0], x, preferred_element_type=F32).astype(BF16)
    gu_ref[0] = jnp.dot(dup_ref[0], x, preferred_element_type=F32).astype(BF16)
    gd_ref[0] = jnp.dot(gated_ref[0], dy, preferred_element_type=F32).astype(BF16)


def per_device(tokens, cotangent, probs, experts, w_gate, w_up, w_down):
    rows, features = tokens.shape
    top = experts.shape[1]
    zs, xs = lax.axis_size("expert"), lax.axis_size("blk")
    cores = lax.axis_size("tensor")
    positions = zs * xs
    half = rows // cores
    halves, _, quarter = w_gate.shape
    span = 2 if halves % 2 == 0 else 1
    count = halves // span
    hidden = span * quarter
    slots = positions * MOST
    core = lax.axis_index("tensor")
    position = lax.axis_index("expert") * xs + lax.axis_index("blk")
    kinds = 8 * pl.cdiv(top, 8)
    barrier = lax.optimization_barrier

    def swap(array):
        return lax.ppermute(array, "tensor", [(i, (i + 1) % cores) for i in range(cores)])

    def along_z(array, by):
        return lax.ppermute(array, "expert", [(i, (i + by) % zs) for i in range(zs)])

    def along_x(array, by):
        return lax.ppermute(array, "blk", [(i, (i + by) % xs) for i in range(xs)])

    def own_first(array):
        return jnp.roll(array, -core * half, axis=-1)

    experts_t = own_first(experts.T)
    probs_t = own_first(probs.T)
    meta = jnp.concatenate(
        [
            jnp.pad(experts_t.astype(BF16), ((0, kinds - top), (0, 0)), constant_values=-1.0),
            jnp.pad(probs_t, ((0, kinds - top), (0, 0))),
        ]
    ).reshape(-1, features)
    meta = jnp.pad(meta, ((0, -meta.shape[0] % 8), (0, 0)))
    own_x = jnp.concatenate([lax.dynamic_slice_in_dim(tokens, core * half, half, 0), meta])
    own_dy = lax.dynamic_slice_in_dim(cotangent, core * half, half, 0)

    line_x = [own_x] + [along_z(own_x, d) for d in range(1, zs)]
    first_x = [along_x(own_x, c) for c in range(1, xs)]
    line_dy = [own_dy]
    for d in range(1, zs):
        send, line_x[d] = barrier((own_dy, line_x[d]))
        line_dy.append(along_z(send, d))
    first_dy = [along_x(own_dy, c) for c in range(1, xs)]
    rest_x = jnp.stack(line_x[1:])
    more_x = [along_x(rest_x, c) for c in range(1, xs)]
    groups_x = [jnp.stack(line_x)] + [jnp.concatenate([a[None], b]) for a, b in zip(first_x, more_x)]
    near_x = jnp.concatenate(groups_x)
    far_x = jnp.concatenate([swap(group) for group in groups_x])
    more_dy = [[along_x(block, c) for block in line_dy[1:]] for c in range(1, xs)]
    near_x, *_ = barrier((near_x, *line_dy[1:]))

    wg = jnp.swapaxes(w_gate, 1, 2).reshape(count, hidden, features)
    wu = jnp.swapaxes(w_up, 1, 2).reshape(count, hidden, features)
    wd = w_down.reshape(count, hidden, features)
    where = jnp.stack([position * halves, lax.axis_index("expert"), lax.axis_index("blk")]).astype(jnp.int32)

    per_step = min(positions, 8)
    steps = positions // per_step
    tall = own_x.shape[0]
    gathering = lambda i: (jnp.minimum(i, steps - 1), 0, 0)
    working = lambda i: (jnp.clip(i - steps, 0, count - 1), 0, 0)
    scalar = pl.BlockSpec(memory_space=pltpu.SMEM)
    weight_spec = pl.BlockSpec((1, hidden, features), working)
    rows_spec = pl.BlockSpec((1, slots, features), working)
    hidden_spec = pl.BlockSpec((1, hidden, slots), working)
    params = pltpu.CompilerParams(vmem_limit_bytes=VMEM_BYTES, dimension_semantics=("arbitrary",))
    flops = 2 * count * hidden * slots * features
    shaped = jax.ShapeDtypeStruct
    x_spec = pl.BlockSpec((per_step, tall, features), gathering)
    table_spec = pl.BlockSpec((per_step * count, rows), lambda i: (jnp.minimum(i, steps - 1), 0))

    rows_x, gate, up, rank, weight, meta_table = pl.pallas_call(
        functools.partial(first_kernel, steps, span, kinds),
        grid=(steps + count,),
        in_specs=[scalar, x_spec, x_spec, weight_spec, weight_spec],
        out_specs=[rows_spec, hidden_spec, hidden_spec, table_spec, table_spec,
                   pl.BlockSpec((per_step, 2 * kinds, rows), gathering)],
        out_shape=[
            shaped((count, slots, features), BF16),
            shaped((count, hidden, slots), F32),
            shaped((count, hidden, slots), F32),
            shaped((positions * count, rows), F32),
            shaped((positions * count, rows), F32),
            shaped((positions, 2 * kinds, rows), F32),
        ],
        scratch_shapes=[pltpu.VMEM((count, slots, features), BF16)],
        compiler_params=params,
        cost_estimate=pl.CostEstimate(flops=2 * flops, bytes_accessed=20_000_000, transcendentals=0),
        name="forward",
    )(where, near_x, far_x, wg, wu)

    more_dy, rank = barrier((more_dy, rank))
    groups_dy = [jnp.stack(line_dy)] + [jnp.stack([a] + b) for a, b in zip(first_dy, more_dy)]
    near_dy = jnp.concatenate(groups_dy)
    far_dy = jnp.concatenate([swap(group) for group in groups_dy])
    dy_spec = pl.BlockSpec((per_step, half, features), gathering)
    back = half + 8 * pl.cdiv(kinds * rows, 8 * features)
    out_spec = pl.BlockSpec((per_step, back, features), lambda i: (jnp.clip(i - steps - count, 0, steps - 1), 0, 0))
    meta_spec = pl.BlockSpec((positions, 2 * kinds, rows), lambda i: (0, 0, 0))
    whole_spec = pl.BlockSpec((positions * count, rows), lambda i: (0, 0))
    rows_dy, dgate, dup, gated, own, other = pl.pallas_call(
        functools.partial(second_kernel, steps, span),
        grid=(steps + count + steps,),
        in_specs=[scalar, whole_spec, whole_spec, meta_spec, dy_spec, dy_spec, weight_spec, weight_spec, weight_spec, hidden_spec,
                  hidden_spec],
        out_specs=[rows_spec, hidden_spec, hidden_spec, hidden_spec, out_spec, out_spec],
        out_shape=[
            shaped((count, slots, features), BF16),
            shaped((count, hidden, slots), BF16),
            shaped((count, hidden, slots), BF16),
            shaped((count, hidden, slots), BF16),
            shaped((positions, back, features), BF16),
            shaped((positions, back, features), BF16),
        ],
        scratch_shapes=[
            pltpu.VMEM((count, slots, features), BF16),
            pltpu.VMEM((count, slots, features), BF16),
            pltpu.VMEM((count, positions, rows), F32),
        ],
        compiler_params=params,
        cost_estimate=pl.CostEstimate(flops=3 * flops, bytes_accessed=30_000_000, transcendentals=0),
        name="backward",
    )(where, rank, weight, meta_table, near_dy, far_dy, wg, wu, wd, gate, up)

    parts = zs if count % zs == 0 else 1
    size = count // parts

    def weights(part, saved, grads):
        at = lambda i: (i + part * size, 0, 0)
        block = lambda height, width: pl.BlockSpec((1, height, width), at)
        return pl.pallas_call(
            third_kernel,
            grid=(size,),
            in_specs=[block(slots, features)] * 2 + [block(hidden, slots)] * 3
            + [pl.BlockSpec(memory_space=pl.ANY)] * len(grads),
            out_specs=[block(hidden, features)] * 3,
            out_shape=[shaped((count, hidden, features), BF16)] * 3,
            input_output_aliases={5 + i: i for i in range(len(grads))},
            compiler_params=params,
            cost_estimate=pl.CostEstimate(flops=3 * flops // parts, bytes_accessed=24_000_000 // parts, transcendentals=0),
            name="weights",
        )(*saved, *grads)

    saved, grads = (rows_x, rows_dy, dgate, dup, gated), ()

    own = own.reshape(xs, zs, back, features)
    other = other.reshape(xs, zs, back, features)
    chip = [None] * xs
    for c in list(range(1, xs)) + [0]:
        chip[c] = (own[c].astype(F32) + swap(other[c]).astype(F32)).astype(BF16)
    turn = list(range(1, zs)) + [0]
    hops = {d: [along_x(chip[c][d], -c) for c in range(1, xs)] for d in turn}
    pieces = []
    for number, d in enumerate(turn):
        total = chip[0][d].astype(F32)
        for hop in hops[d]:
            total = total + hop.astype(F32)
        if d:
            total = total.astype(BF16)
            pieces.append(along_z(total, -d))
        if number < parts:
            total, saved = barrier((total, saved))
            grads = weights(number, saved, grads)
            if number + 1 < len(turn):
                follow = turn[number + 1]
                hops[follow], grads = barrier((hops[follow], grads))
    for piece in pieces:
        total = total + piece.astype(F32)
    mine = total.astype(BF16)
    theirs = swap(mine)

    def tokens_of(piece):
        return piece[:half]

    def probs_of(piece):
        return piece[half:].reshape(-1)[: kinds * rows].reshape(kinds, rows)[:top, :half].astype(F32)

    def in_order(part, axis):
        both = part(mine), part(theirs)
        return jnp.where(core == 0, jnp.concatenate(both, axis), jnp.concatenate(both[::-1], axis))

    grad_tokens = in_order(tokens_of, 0)
    grad_probs = in_order(probs_of, 1).T
    grad_gate, grad_up, grad_down = grads
    shape = (halves, quarter, features)
    return (
        grad_tokens,
        grad_probs,
        jnp.swapaxes(grad_gate.reshape(shape), 1, 2),
        jnp.swapaxes(grad_up.reshape(shape), 1, 2),
        grad_down.reshape(shape),
    )


def solution(mesh):
    return jax.shard_map(
        per_device,
        mesh=mesh,
        in_specs=(
            P(("groups", "expert", "blk"), None),
            P(("groups", "expert", "blk"), None),
            P(("groups", "expert", "blk"), None),
            P(("groups", "expert", "blk"), None),
            P(("expert", "blk"), None, "tensor"),
            P(("expert", "blk"), None, "tensor"),
            P(("expert", "blk"), "tensor", None),
        ),
        out_specs=(
            P(("groups", "expert", "blk"), None),
            P(("groups", "expert", "blk"), None),
            P(("groups", "expert", "blk"), None, "tensor"),
            P(("groups", "expert", "blk"), None, "tensor"),
            P(("groups", "expert", "blk"), "tensor", None),
        ),
        check_vma=False,
    )
```

```python
import functools

import jax
import jax.numpy as jnp
from jax import lax
from jax.experimental import pallas as pl
from jax.experimental.pallas import tpu as pltpu
from jax.sharding import PartitionSpec as P

MOST = 16
BF16, F32 = jnp.bfloat16, jnp.float32
LAST = (((1,), (1,)), ((), ()))
LEAD = (((0,), (0,)), ((), ()))
VMEM_BYTES = 12 * 1024 * 1024


def cost(micros):
    return pl.CostEstimate(flops=1000, bytes_accessed=int(micros * 3_000_000), transcendentals=0)


def dot(a, b, dims):
    return lax.dot_general(a, b, dims, preferred_element_type=F32)


def iota(shape, dim):
    return lax.broadcasted_iota(jnp.int32, shape, dim)


def ranks_and_probs(first, meta, span, count):
    sources, height, tokens = meta.shape
    kinds = height // 2
    wanted = ((first + span * iota((count, tokens), 0)) >> 1).astype(F32)
    named, weight = [], []
    for source in range(sources):
        entry = meta[source].astype(F32)
        hit = jnp.zeros((count, tokens), F32)
        prob = jnp.zeros((count, tokens), F32)
        for kind in range(kinds):
            same = entry[kind : kind + 1] == wanted
            hit = jnp.where(same, 1.0, hit)
            prob = jnp.where(same, entry[kinds + kind : kinds + kind + 1], prob)
        named.append(hit)
        weight.append(prob)
    named = jnp.concatenate(named)
    before = (iota((tokens, tokens), 0) < iota((tokens, tokens), 1)).astype(F32).astype(BF16)
    rank = jnp.dot(named.astype(BF16), before, preferred_element_type=F32)
    return jnp.where(named > 0, rank, -1.0), jnp.concatenate(weight)


def slot_matrix(rank):
    count, tokens = rank.shape
    wide = jnp.broadcast_to(rank[:, None, :], (count, MOST, tokens)).reshape(count * MOST, tokens)
    place = (iota((count * MOST, tokens), 0) & (MOST - 1)).astype(F32)
    return jnp.where(wide == place, 1.0, 0.0).astype(BF16)


def select(rank, near, far, rows_ref):
    count, _, features = rows_ref.shape
    sources = near.shape[0]
    half = rank.shape[1] // 2
    for source in range(sources):
        pick = slot_matrix(rank[source * count : (source + 1) * count])
        both = jnp.concatenate([near[source, :half], far[source, :half]], axis=0)
        rows = jnp.dot(pick, both, preferred_element_type=F32).astype(BF16)
        rows_ref[:, source * MOST : (source + 1) * MOST, :] = rows.reshape(count, MOST, features)


def select_tokens(span, kinds, where_ref, near_ref, far_ref, rows_ref, rank_ref, weight_ref, meta_ref):
    tokens = rank_ref.shape[1]
    half, per_row = tokens // 2, near_ref.shape[2] // tokens
    lines = []
    for number in range(2 * kinds):
        at, part = half + number // per_row, number % per_row
        lines.append(near_ref[:, at : at + 1, part * tokens : (part + 1) * tokens].astype(F32))
    meta = jnp.concatenate(lines, axis=1)
    rank, weight = ranks_and_probs(where_ref[0], meta, span, rows_ref.shape[0])
    rank_ref[...] = rank
    weight_ref[...] = weight
    meta_ref[...] = meta
    select(rank, near_ref, far_ref, rows_ref)


def select_cotangents(where_ref, rank_ref, near_ref, far_ref, rows_ref):
    select(rank_ref[...], near_ref, far_ref, rows_ref)


def joined(refs, index):
    return jnp.concatenate([ref[index] for ref in refs], axis=0)


def each(count, body):
    def step(index, carry):
        body(index)
        return carry

    lax.fori_loop(0, count, step, 0, unroll=2 if count % 2 == 0 else 1)


def forward_kernel(where_ref, wg_ref, wu_ref, *refs):
    rows_refs, (gate_ref, up_ref) = refs[:-2], refs[-2:]

    def body(expert):
        rows = joined(rows_refs, expert)
        gate_ref[expert] = dot(wg_ref[expert], rows, LAST)
        up_ref[expert] = dot(wu_ref[expert], rows, LAST)

    each(gate_ref.shape[0], body)


def backward_kernel(groups, where_ref, wg_ref, wu_ref, wd_ref, gate_ref, up_ref, *refs):
    rank_refs, weight_refs, rows_refs = refs[:groups], refs[groups : 2 * groups], refs[2 * groups : 3 * groups]
    dgate_ref, dup_ref, gated_ref, input_ref, prob_ref = refs[3 * groups :]
    count, slots, _ = input_ref.shape
    sources, tokens = prob_ref.shape[1:]
    total = sources * count
    rank = joined(rank_refs, ...).astype(BF16)
    weight = joined(weight_refs, ...).astype(BF16)
    place = (iota((tokens, slots), 1) & (MOST - 1)).astype(F32)
    row, lane = iota((total, slots), 0), iota((total, slots), 1)
    block = jnp.where(iota((sources, slots), 0) == iota((sources, slots), 1) // MOST, 1.0, 0.0).astype(BF16)

    def body(expert):
        spread = jnp.where(row == (lane // MOST) * count + expert, 1.0, 0.0).astype(BF16)
        holds = dot(rank, spread, LEAD) == place
        scale = jnp.sum(jnp.where(holds, dot(weight, spread, LEAD), 0.0), axis=0, keepdims=True)
        raw = dot(wd_ref[expert], joined(rows_refs, expert), LAST)
        gate, up = gate_ref[expert], up_ref[expert]
        sigmoid = 1.0 / (1.0 + jnp.exp(-gate))
        active = gate * sigmoid
        hidden = active * up
        gated_ref[expert] = (scale * hidden).astype(BF16)
        prob = jnp.sum(hidden * raw, axis=0, keepdims=True)
        scaled = scale * raw
        dgate = (scaled * up * sigmoid * (1.0 + gate * (1.0 - sigmoid))).astype(BF16)
        dup = (scaled * active).astype(BF16)
        dgate_ref[expert] = dgate
        dup_ref[expert] = dup
        input_ref[expert] = (dot(dgate, wg_ref[expert], LEAD) + dot(dup, wu_ref[expert], LEAD)).astype(BF16)
        prob_ref[expert] = dot(block, jnp.where(holds, prob, 0.0).astype(BF16), LAST)

    each(count, body)


def put_back(span, base, where_ref, rank_ref, meta_ref, input_ref, prob_ref, own_ref, other_ref):
    count, _, features = input_ref.shape
    tokens = rank_ref.shape[1]
    half, per_row = tokens // 2, features // tokens
    kinds = meta_ref.shape[1] // 2
    tail = own_ref.shape[1] - half
    wanted = ((where_ref[0] + span * iota((count, tokens), 0)) >> 1).astype(F32)
    for source in range(own_ref.shape[0]):
        number = base + source
        pick = slot_matrix(rank_ref[source * count : (source + 1) * count])
        rows = input_ref[:, number * MOST : (number + 1) * MOST, :].reshape(count * MOST, features)
        part = dot(pick, rows, LEAD).astype(BF16)
        own_ref[source, :half] = part[:half]
        other_ref[source, :half] = part[half:]
        prob = prob_ref[:, number, :]
        entry = meta_ref[source]
        line = [
            jnp.sum(jnp.where(entry[kind : kind + 1] == wanted, prob, 0.0), axis=0, keepdims=True)
            for kind in range(kinds)
        ]
        flip = [pltpu.roll(jnp.broadcast_to(row, (8, tokens)), half, 1)[:1] for row in line]
        for ref, parts in ((own_ref, line), (other_ref, flip)):
            lines = [jnp.concatenate(parts[at : at + per_row], axis=1) for at in range(0, kinds, per_row)]
            lines += [jnp.zeros_like(lines[0])] * (tail - len(lines))
            ref[source, half:] = jnp.concatenate(lines, axis=0).astype(BF16)


def weights_kernel(groups, where_ref, dgate_ref, dup_ref, gated_ref, *refs):
    rows_x, rows_dy = refs[:groups], refs[groups : 2 * groups]
    targets, token_ref = refs[2 * groups : 2 * groups + 3], refs[2 * groups + 3]
    slots_ref, sems = refs[2 * groups + 4 :]
    count, depth = dgate_ref.shape[0], slots_ref.shape[0]

    def copies(expert):
        slot = lax.rem(expert, depth)
        return [
            pltpu.make_async_copy(slots_ref.at[slot, number], target.at[expert], sems.at[slot, number])
            for number, target in enumerate(targets)
        ]

    def body(expert, carry):
        @pl.when(expert >= depth)
        def _():
            for copy in copies(expert - depth):
                copy.wait()

        slot = lax.rem(expert, depth)
        x, dy = joined(rows_x, expert), joined(rows_dy, expert)
        slots_ref[slot, 0] = jnp.dot(dgate_ref[expert], x, preferred_element_type=F32).astype(BF16)
        slots_ref[slot, 1] = jnp.dot(dup_ref[expert], x, preferred_element_type=F32).astype(BF16)
        slots_ref[slot, 2] = jnp.dot(gated_ref[expert], dy, preferred_element_type=F32).astype(BF16)
        for copy in copies(expert):
            copy.start()
        return carry

    lax.fori_loop(0, count, body, 0)
    for expert in range(max(count - depth, 0), count):
        for copy in copies(expert):
            copy.wait()
    pass_on(where_ref, token_ref)


def line_sums(places, peers, keep, where_ref, own_ref, other_ref, *refs):
    hops, outs = refs[:peers], refs[peers:]
    for at, (place, out) in enumerate(zip(places, outs)):
        total = own_ref[place].astype(F32) + other_ref[place].astype(F32)
        for hop in hops:
            total = total + hop[at].astype(F32)
        out[...] = total if place == keep else total.astype(BF16)


def last_sum(where_ref, kept_ref, *refs):
    total = kept_ref[...]
    for piece in refs[:-1]:
        total = total + piece[...].astype(F32)
    refs[-1][...] = total.astype(BF16)


def in_vmem(array):
    return pltpu.with_memory_space_constraint(array, pltpu.VMEM)


def in_hbm(array):
    return pltpu.with_memory_space_constraint(array, pltpu.HBM)


def vmem_shape(shape, dtype):
    return pltpu.VMEM(shape, dtype)


def in_hbm(array):
    return pltpu.with_memory_space_constraint(array, pltpu.HBM)


def vmem_shape(shape, dtype):
    return pltpu.VMEM(shape, dtype)


def pass_on(where_ref, token_ref):
    for number in range(3):
        token_ref[number] = where_ref[number]


def load_kernel(where_ref, *refs):
    count = (len(refs) - 2) // 2
    token_ref, sems = refs[2 * count :]
    copies = [
        pltpu.make_async_copy(source, target, sems.at[number])
        for number, (source, target) in enumerate(zip(refs[:count], refs[count : 2 * count]))
    ]
    for copy in copies:
        copy.start()
    for copy in copies:
        copy.wait()
    pass_on(where_ref, token_ref)


SCALARS = pl.BlockSpec(memory_space=pltpu.SMEM)
IN_VMEM = pl.BlockSpec(memory_space=pltpu.VMEM)
TOKEN = jax.ShapeDtypeStruct((3,), jnp.int32)


def load(where, arrays):
    *held, where = pl.pallas_call(
        load_kernel,
        in_specs=[SCALARS] + [pl.BlockSpec(memory_space=pl.ANY)] * len(arrays),
        out_specs=[IN_VMEM] * len(arrays) + [SCALARS],
        out_shape=[vmem_shape(array.shape, array.dtype) for array in arrays] + [TOKEN],
        scratch_shapes=[pltpu.SemaphoreType.DMA((len(arrays),))],
        compiler_params=pltpu.CompilerParams(vmem_limit_bytes=VMEM_BYTES),
        cost_estimate=cost(7),
        name="load",
    )(where, *map(in_hbm, arrays))
    return where, held


def on_vmem(kernel, name, micros, outs, where, operands, stay=True):
    def body(where_ref, *refs):
        kernel(where_ref, *refs[:-1])
        pass_on(where_ref, refs[-1])

    *held, where = pl.pallas_call(
        body,
        in_specs=[SCALARS] + [IN_VMEM] * len(operands),
        out_specs=[IN_VMEM] * len(outs) + [SCALARS],
        out_shape=[(vmem_shape if stay else jax.ShapeDtypeStruct)(shape, dtype) for shape, dtype in outs] + [TOKEN],
        compiler_params=pltpu.CompilerParams(vmem_limit_bytes=VMEM_BYTES),
        cost_estimate=cost(micros),
        name=name,
    )(where, *map(in_vmem, operands))
    return where, held


def per_device(tokens, cotangent, probs, experts, w_gate, w_up, w_down):
    rows, features = tokens.shape
    top = experts.shape[1]
    zs, xs = lax.axis_size("expert"), lax.axis_size("blk")
    cores = lax.axis_size("tensor")
    positions = zs * xs
    half = rows // cores
    halves, _, quarter = w_gate.shape
    span = 2 if halves % 2 == 0 else 1
    count = halves // span
    hidden = span * quarter
    slots = positions * MOST
    core = lax.axis_index("tensor")
    position = lax.axis_index("expert") * xs + lax.axis_index("blk")
    kinds = 8 * pl.cdiv(top, 8)
    barrier = lax.optimization_barrier

    def swap(array):
        return lax.ppermute(array, "tensor", [(i, (i + 1) % cores) for i in range(cores)])

    def along_z(array, by):
        return lax.ppermute(array, "expert", [(i, (i + by) % zs) for i in range(zs)])

    def along_x(array, by):
        return lax.ppermute(array, "blk", [(i, (i + by) % xs) for i in range(xs)])

    def own_first(array):
        return jnp.roll(array, -core * half, axis=-1)

    experts_t = own_first(experts.T)
    probs_t = own_first(probs.T)
    meta = jnp.concatenate(
        [
            jnp.pad(experts_t.astype(BF16), ((0, kinds - top), (0, 0)), constant_values=-1.0),
            jnp.pad(probs_t, ((0, kinds - top), (0, 0))),
        ]
    ).reshape(-1, features)
    meta = jnp.pad(meta, ((0, -meta.shape[0] % 8), (0, 0)))
    own_x = jnp.concatenate([lax.dynamic_slice_in_dim(tokens, core * half, half, 0), meta])
    own_dy = lax.dynamic_slice_in_dim(cotangent, core * half, half, 0)

    wg = jnp.swapaxes(w_gate, 1, 2).reshape(count, hidden, features)
    wu = jnp.swapaxes(w_up, 1, 2).reshape(count, hidden, features)
    wd = w_down.reshape(count, hidden, features)
    where = jnp.stack([position * halves, lax.axis_index("expert"), lax.axis_index("blk")]).astype(jnp.int32)
    group = zs * MOST

    line_x = [along_z(own_x, d) for d in range(1, zs)]
    first_x = [along_x(own_x, c) for c in range(1, xs)]
    first_dy = [along_x(own_dy, c) for c in range(1, xs)]
    where, own_x = barrier((where, own_x))
    where, (wg, wu, wd) = load(where, (wg, wu, wd))
    where, line_x, first_x, first_dy, own_dy = barrier((where, line_x, first_x, first_dy, own_dy))

    line_dy = [along_z(own_dy, d) for d in range(1, zs)]
    rest = jnp.stack(line_x)
    more = [along_x(rest, c) for c in range(1, xs)]
    rows_x, ranks, weight, metas = [], [], [], []

    def take_tokens(where, near, far):
        outs = [((count, group, features), BF16), ((zs * count, rows), F32), ((zs * count, rows), F32),
                ((zs, 2 * kinds, rows), F32)]
        where, results = on_vmem(functools.partial(select_tokens, span, kinds), "select_tokens", 2, outs, where, (near, far))
        for held, result in zip((rows_x, ranks, weight, metas), results):
            held.append(result)
        return where

    def take_cotangents(where, near, far):
        outs = [((count, group, features), BF16)]
        return on_vmem(select_cotangents, "select_cotangents", 2, outs, where, (ranks[len(rows_dy)], near, far))

    near = jnp.concatenate([own_x[None], rest])
    where = take_tokens(where, near, swap(near))
    where, line_dy, more = barrier((where, line_dy, more))
    groups_x = [jnp.concatenate([a[None], b]) for a, b in zip(first_x, more)]

    rest = jnp.stack(line_dy)
    more = [along_x(rest, c) for c in range(1, xs)]
    rows_dy = []
    for near in groups_x:
        where = take_tokens(where, near, swap(near))
    where, (gate, up) = on_vmem(forward_kernel, "forward", 5, [((count, hidden, slots), F32)] * 2, where, (wg, wu, *rows_x))
    near = jnp.concatenate([own_dy[None], rest])
    where, got = take_cotangents(where, near, swap(near))
    rows_dy += got
    where, more = barrier((where, more))
    for near in [jnp.concatenate([a[None], b]) for a, b in zip(first_dy, more)]:
        where, got = take_cotangents(where, near, swap(near))
        rows_dy += got

    outs = [((count, hidden, slots), BF16)] * 3 + [((count, slots, features), BF16), ((count, positions, rows), F32)]
    where, (dgate, dup, gated, rows_in, prob) = on_vmem(
        functools.partial(backward_kernel, xs), "backward", 9, outs, where,
        (wg, wu, wd, gate, up, *ranks, *weight, *rows_dy))
    back = half + 8 * pl.cdiv(kinds * rows, 8 * features)
    chip = [None] * xs
    for c in list(range(1, xs)) + [0]:
        where, (own, other) = on_vmem(
            functools.partial(put_back, span, c * zs), "put_back", 2, [((zs, back, features), BF16)] * 2, where,
            (ranks[c], metas[c], rows_in, prob), False)
        chip[c] = own, swap(other)
    sums = [None] + [(own.astype(F32) + other.astype(F32)).astype(BF16) for own, other in chip[1:]]
    saved = (dgate, dup, gated, *rows_x, *rows_dy)

    def weights(where):
        depth = min(count, 2)
        *grads, where = pl.pallas_call(
            functools.partial(weights_kernel, xs),
            in_specs=[SCALARS] + [IN_VMEM] * len(saved),
            out_specs=[pl.BlockSpec(memory_space=pl.ANY)] * 3 + [SCALARS],
            out_shape=[jax.ShapeDtypeStruct((count, hidden, features), BF16)] * 3 + [TOKEN],
            scratch_shapes=[pltpu.VMEM((depth, 3, hidden, features), BF16), pltpu.SemaphoreType.DMA((depth, 3))],
            compiler_params=pltpu.CompilerParams(vmem_limit_bytes=VMEM_BYTES),
            cost_estimate=cost(9),
            name="weights",
        )(where, *map(in_vmem, saved))
        return where, grads

    turn = list(range(1, zs)) + [0]
    turns = [turn[: zs // 2], turn[zs // 2 :]]
    hops = [[along_x(jnp.stack([sums[c][d] for d in some]), -c) for c in range(1, xs)] for some in turns]
    where, grads = weights(where)
    pieces = []
    for some, hop in zip(turns, hops):
        outs = [((back, features), BF16 if d else F32) for d in some]
        where, parts = on_vmem(functools.partial(line_sums, some, len(hop), 0), "line_sums", 1, outs, where,
                               (*chip[0], *hop), False)
        pieces += [along_z(part, -d) if d else part for d, part in zip(some, parts)]
    where, (mine,) = on_vmem(last_sum, "last_sum", 1, [((back, features), BF16)], where, pieces[::-1], False)
    theirs = swap(mine)

    def tokens_of(piece):
        return piece[:half]

    def probs_of(piece):
        return piece[half:].reshape(-1)[: kinds * rows].reshape(kinds, rows)[:top, :half].astype(F32)

    def in_order(part, axis):
        both = part(mine), part(theirs)
        return jnp.where(core == 0, jnp.concatenate(both, axis), jnp.concatenate(both[::-1], axis))

    grad_tokens = in_order(tokens_of, 0)
    grad_probs = in_order(probs_of, 1).T
    grad_gate, grad_up, grad_down = grads
    shape = (halves, quarter, features)
    return (
        grad_tokens,
        grad_probs,
        jnp.swapaxes(grad_gate.reshape(shape), 1, 2),
        jnp.swapaxes(grad_up.reshape(shape), 1, 2),
        grad_down.reshape(shape),
    )


def solution(mesh):
    return jax.shard_map(
        per_device,
        mesh=mesh,
        in_specs=(
            P(("groups", "expert", "blk"), None),
            P(("groups", "expert", "blk"), None),
            P(("groups", "expert", "blk"), None),
            P(("groups", "expert", "blk"), None),
            P(("expert", "blk"), None, "tensor"),
            P(("expert", "blk"), None, "tensor"),
            P(("expert", "blk"), "tensor", None),
        ),
        out_specs=(
            P(("groups", "expert", "blk"), None),
            P(("groups", "expert", "blk"), None),
            P(("groups", "expert", "blk"), None, "tensor"),
            P(("groups", "expert", "blk"), None, "tensor"),
            P(("groups", "expert", "blk"), "tensor", None),
        ),
        check_vma=False,
    )
```

```python
import functools

import jax
import jax.numpy as jnp
from jax import lax
from jax.experimental import pallas as pl
from jax.experimental.pallas import tpu as pltpu
from jax.sharding import PartitionSpec as P

MOST = 16
BF16, F32 = jnp.bfloat16, jnp.float32
LAST = (((1,), (1,)), ((), ()))
LEAD = (((0,), (0,)), ((), ()))
VMEM_BYTES = 12 * 1024 * 1024


def cost(micros):
    return pl.CostEstimate(flops=1000, bytes_accessed=int(micros * 3_000_000), transcendentals=0)


def dot(a, b, dims):
    return lax.dot_general(a, b, dims, preferred_element_type=F32)


def iota(shape, dim):
    return lax.broadcasted_iota(jnp.int32, shape, dim)


def ranks_and_probs(first, meta, span, count):
    sources, height, tokens = meta.shape
    kinds = height // 2
    wanted = ((first + span * iota((count, tokens), 0)) >> 1).astype(F32)
    named, weight = [], []
    for source in range(sources):
        entry = meta[source].astype(F32)
        hit = jnp.zeros((count, tokens), F32)
        prob = jnp.zeros((count, tokens), F32)
        for kind in range(kinds):
            same = entry[kind : kind + 1] == wanted
            hit = jnp.where(same, 1.0, hit)
            prob = jnp.where(same, entry[kinds + kind : kinds + kind + 1], prob)
        named.append(hit)
        weight.append(prob)
    named = jnp.concatenate(named)
    before = (iota((tokens, tokens), 0) < iota((tokens, tokens), 1)).astype(F32).astype(BF16)
    rank = jnp.dot(named.astype(BF16), before, preferred_element_type=F32)
    return jnp.where(named > 0, rank, -1.0), jnp.concatenate(weight)


def slot_matrix(rank):
    count, tokens = rank.shape
    wide = jnp.broadcast_to(rank[:, None, :], (count, MOST, tokens)).reshape(count * MOST, tokens)
    place = (iota((count * MOST, tokens), 0) & (MOST - 1)).astype(F32)
    return jnp.where(wide == place, 1.0, 0.0).astype(BF16)


def select(rank, near, far, rows_ref):
    count, sources = rows_ref.shape[0], rows_ref.shape[1] // MOST
    for source in range(sources):
        pick = slot_matrix(rank[source * count : (source + 1) * count])
        both = jnp.concatenate([near(source), far(source)], axis=0)
        rows = jnp.dot(pick, both, preferred_element_type=F32).astype(BF16)
        rows_ref[:, source * MOST : (source + 1) * MOST, :] = rows.reshape(count, MOST, rows.shape[1])


def unpacked(piece, half, features):
    chunks = features // piece.shape[1]
    return jnp.concatenate([piece[chunk * half : (chunk + 1) * half] for chunk in range(chunks)], axis=1)


def store_packed(ref, index, rows):
    half, features = rows.shape
    lanes = ref.shape[-1]
    for chunk in range(features // lanes):
        ref[(*index, slice(chunk * half, (chunk + 1) * half))] = rows[:, chunk * lanes : (chunk + 1) * lanes]


def pack(where_ref, tokens_ref, cotangent_ref, experts_ref, probs_ref, x_ref, dy_ref, token_ref, half_scr, experts_scr,
         chosen_scr, ids_scr, prob_scr, sems):
    second = where_ref[1] == 1
    half = dy_ref.shape[0]
    top, kinds = experts_ref.shape[0], ids_scr.shape[0]
    mine = pl.ds(pl.multiple_of(where_ref[1] * half, half), half)
    pairs = ((tokens_ref.at[mine], half_scr), (experts_ref, experts_scr), (probs_ref, chosen_scr),
             (cotangent_ref.at[mine], dy_ref))
    copies = [pltpu.make_async_copy(source, target, sems.at[at]) for at, (source, target) in enumerate(pairs)]
    for copy in copies:
        copy.start()
    pass_on(where_ref, token_ref)
    for copy in copies:
        copy.wait()
    store_packed(x_ref, (), half_scr[...])
    ids_scr[...] = jnp.full(ids_scr.shape, -1.0, F32)
    prob_scr[...] = jnp.zeros(prob_scr.shape, F32)
    ids_scr[:top] = experts_scr[...].astype(F32)
    prob_scr[:top] = chosen_scr[...].astype(F32)
    lines = [jnp.where(second, pltpu.roll(ref[...], half, 1), ref[...]) for ref in (ids_scr, prob_scr)]
    x_ref[x_ref.shape[0] - 2 * kinds :] = jnp.concatenate(lines, axis=0).astype(BF16)


def select_tokens(span, where_ref, near_ref, far_ref, rows_ref, rank_ref, weight_ref, meta_ref):
    half, features, height = rank_ref.shape[1] // 2, rows_ref.shape[2], meta_ref.shape[1]
    meta = near_ref[:, near_ref.shape[1] - height :, :].astype(F32)
    rank, weight = ranks_and_probs(where_ref[0], meta, span, rows_ref.shape[0])
    rank_ref[...] = rank
    weight_ref[...] = weight
    meta_ref[...] = meta
    select(rank, lambda source: unpacked(near_ref[source], half, features),
           lambda source: unpacked(far_ref[source], half, features), rows_ref)


def select_cotangents(where_ref, rank_ref, near_ref, far_ref, rows_ref):
    select(rank_ref[...], lambda source: near_ref[source], lambda source: far_ref[source], rows_ref)


def joined(refs, index):
    return jnp.concatenate([ref[index] for ref in refs], axis=0)


def each(count, body):
    def step(index, carry):
        body(index)
        return carry

    lax.fori_loop(0, count, step, 0, unroll=2 if count % 2 == 0 else 1)


def forward_kernel(where_ref, wg_ref, wu_ref, *refs):
    rows_refs, (gate_ref, up_ref) = refs[:-2], refs[-2:]

    def body(expert):
        rows = joined(rows_refs, expert)
        gate_ref[expert] = dot(wg_ref[expert], rows, LAST)
        up_ref[expert] = dot(wu_ref[expert], rows, LAST)

    each(gate_ref.shape[0], body)


def backward_kernel(groups, where_ref, wg_ref, wu_ref, wd_ref, gate_ref, up_ref, *refs):
    rank_refs, weight_refs, rows_refs = refs[:groups], refs[groups : 2 * groups], refs[2 * groups : 3 * groups]
    dgate_ref, dup_ref, gated_ref, input_ref, prob_ref = refs[3 * groups :]
    count, slots, _ = input_ref.shape
    sources, tokens = prob_ref.shape[1:]
    total = sources * count
    rank = joined(rank_refs, ...).astype(BF16)
    weight = joined(weight_refs, ...).astype(BF16)
    place = (iota((tokens, slots), 1) & (MOST - 1)).astype(F32)
    row, lane = iota((total, slots), 0), iota((total, slots), 1)
    block = jnp.where(iota((sources, slots), 0) == iota((sources, slots), 1) // MOST, 1.0, 0.0).astype(BF16)

    def body(expert):
        spread = jnp.where(row == (lane // MOST) * count + expert, 1.0, 0.0).astype(BF16)
        holds = dot(rank, spread, LEAD) == place
        scale = jnp.sum(jnp.where(holds, dot(weight, spread, LEAD), 0.0), axis=0, keepdims=True)
        raw = dot(wd_ref[expert], joined(rows_refs, expert), LAST)
        gate, up = gate_ref[expert], up_ref[expert]
        sigmoid = 1.0 / (1.0 + jnp.exp(-gate))
        active = gate * sigmoid
        hidden = active * up
        gated_ref[expert] = (scale * hidden).astype(BF16)
        prob = jnp.sum(hidden * raw, axis=0, keepdims=True)
        scaled = scale * raw
        dgate = (scaled * up * sigmoid * (1.0 + gate * (1.0 - sigmoid))).astype(BF16)
        dup = (scaled * active).astype(BF16)
        dgate_ref[expert] = dgate
        dup_ref[expert] = dup
        input_ref[expert] = (dot(dgate, wg_ref[expert], LEAD) + dot(dup, wu_ref[expert], LEAD)).astype(BF16)
        prob_ref[expert] = dot(block, jnp.where(holds, prob, 0.0).astype(BF16), LAST)

    each(count, body)


def put_back(span, base, where_ref, rank_ref, meta_ref, input_ref, prob_ref, own_ref, other_ref):
    count, _, features = input_ref.shape
    tokens = rank_ref.shape[1]
    half, kinds = tokens // 2, meta_ref.shape[1] // 2
    tail = own_ref.shape[1] - features // own_ref.shape[2] * half
    wanted = ((where_ref[0] + span * iota((count, tokens), 0)) >> 1).astype(F32)
    for source in range(own_ref.shape[0]):
        number = base + source
        pick = slot_matrix(rank_ref[source * count : (source + 1) * count])
        rows = input_ref[:, number * MOST : (number + 1) * MOST, :].reshape(count * MOST, features)
        part = dot(pick, rows, LEAD).astype(BF16)
        store_packed(own_ref, (source,), part[:half])
        store_packed(other_ref, (source,), part[half:])
        prob = prob_ref[:, number, :]
        entry = meta_ref[source]
        lines = jnp.zeros((tail, tokens), F32)
        for kind in range(kinds):
            line = jnp.sum(jnp.where(entry[kind : kind + 1] == wanted, prob, 0.0), axis=0, keepdims=True)
            lines = jnp.where(iota((tail, tokens), 0) == kind, line, lines)
        own_ref[source, own_ref.shape[1] - tail :] = lines.astype(BF16)
        other_ref[source, own_ref.shape[1] - tail :] = pltpu.roll(lines, half, 1).astype(BF16)


def weights_kernel(groups, where_ref, dgate_ref, dup_ref, gated_ref, *refs):
    rows_x, rows_dy = refs[:groups], refs[groups : 2 * groups]
    targets, token_ref, slots_ref, sems = refs[-6:-3], *refs[-3:]
    count, depth = dgate_ref.shape[0], slots_ref.shape[0]

    def copies(expert):
        slot = lax.rem(expert, depth)
        return [
            pltpu.make_async_copy(slots_ref.at[slot, number], target.at[expert], sems.at[slot, number])
            for number, target in enumerate(targets)
        ]

    def body(expert, carry):
        @pl.when(expert >= depth)
        def _():
            for copy in copies(expert - depth):
                copy.wait()

        slot = lax.rem(expert, depth)
        x, dy = joined(rows_x, expert), joined(rows_dy, expert)
        slots_ref[slot, 0] = jnp.dot(dgate_ref[expert], x, preferred_element_type=F32).astype(BF16)
        slots_ref[slot, 1] = jnp.dot(dup_ref[expert], x, preferred_element_type=F32).astype(BF16)
        slots_ref[slot, 2] = jnp.dot(gated_ref[expert], dy, preferred_element_type=F32).astype(BF16)
        for copy in copies(expert):
            copy.start()
        return carry

    lax.fori_loop(0, count, body, 0)
    for expert in range(max(count - depth, 0), count):
        for copy in copies(expert):
            copy.wait()
    pass_on(where_ref, token_ref)


def middle_sums(zs, xs, where_ref, own_ref, other_ref, base_ref, *refs):
    hops, shifts, outs = refs[: xs - 1], refs[xs - 1 : xs + zs - 2], refs[xs + zs - 2 :]
    size = hops[0].shape[1]
    for place in range(zs):
        total = own_ref[place, :size].astype(F32) + other_ref[place, :size].astype(F32)
        for hop in hops:
            total = total + hop[place].astype(F32)
        outs[place][...] = total.astype(outs[place].dtype)
    for place in range(xs):
        total = base_ref[place]
        for piece in shifts:
            total = total + piece[place].astype(F32)
        outs[zs + place][...] = total.astype(outs[zs + place].dtype)


def last_sums(zs, xs, where_ref, *refs):
    first, last, out = refs[:zs], refs[zs : zs + xs], refs[-1]
    size = first[0].shape[0]
    for refs, rows in ((first, slice(0, size)), (last, slice(size, out.shape[0]))):
        total = refs[0][...]
        for ref in refs[1:]:
            total = total + ref[...].astype(F32)
        out[rows] = total.astype(BF16)


def unpack(where_ref, mine_ref, theirs_ref, tokens_ref, probs_ref):
    second = where_ref[1] == 1
    mine, theirs = mine_ref[...], theirs_ref[...]
    half, features = tokens_ref.shape[0] // 2, tokens_ref.shape[1]
    low, high = jnp.where(second, theirs, mine), jnp.where(second, mine, theirs)
    tokens_ref[:half] = unpacked(low, half, features)
    tokens_ref[half:] = unpacked(high, half, features)
    at = features // low.shape[1] * half
    low, high = low[at:].astype(F32), high[at:].astype(F32)
    both = jnp.where(iota(low.shape, 1) < half, low, pltpu.roll(high, half, 1))
    probs_ref[...] = both[: probs_ref.shape[0]]


def in_vmem(array):
    return pltpu.with_memory_space_constraint(array, pltpu.VMEM)


def in_hbm(array):
    return pltpu.with_memory_space_constraint(array, pltpu.HBM)


def vmem_shape(shape, dtype):
    return pltpu.VMEM(shape, dtype)


def in_hbm(array):
    return pltpu.with_memory_space_constraint(array, pltpu.HBM)


def vmem_shape(shape, dtype):
    return pltpu.VMEM(shape, dtype)


def pass_on(where_ref, token_ref):
    for number in range(2):
        token_ref[number] = where_ref[number]


def load_kernel(where_ref, *refs):
    count = (len(refs) - 2) // 2
    token_ref, sems = refs[2 * count :]
    copies = [
        pltpu.make_async_copy(source, target, sems.at[number])
        for number, (source, target) in enumerate(zip(refs[:count], refs[count : 2 * count]))
    ]
    for copy in copies:
        copy.start()
    for copy in copies:
        copy.wait()
    pass_on(where_ref, token_ref)


SCALARS = pl.BlockSpec(memory_space=pltpu.SMEM)
IN_VMEM = pl.BlockSpec(memory_space=pltpu.VMEM)
TOKEN = jax.ShapeDtypeStruct((2,), jnp.int32)


def load(where, arrays):
    *held, where = pl.pallas_call(
        load_kernel,
        in_specs=[SCALARS] + [pl.BlockSpec(memory_space=pl.ANY)] * len(arrays),
        out_specs=[IN_VMEM] * len(arrays) + [SCALARS],
        out_shape=[vmem_shape(array.shape, array.dtype) for array in arrays] + [TOKEN],
        scratch_shapes=[pltpu.SemaphoreType.DMA((len(arrays),))],
        compiler_params=pltpu.CompilerParams(vmem_limit_bytes=VMEM_BYTES),
        cost_estimate=cost(7),
        name="load",
    )(where, *map(in_hbm, arrays))
    return where, held


def on_vmem(kernel, name, micros, outs, where, operands, stay=True, scratch=()):
    def body(where_ref, *refs):
        at = len(operands) + len(outs)
        kernel(where_ref, *refs[:at], *refs[at + 1 :])
        pass_on(where_ref, refs[at])

    *held, where = pl.pallas_call(
        body,
        in_specs=[SCALARS] + [IN_VMEM] * len(operands),
        out_specs=[IN_VMEM] * len(outs) + [SCALARS],
        out_shape=[(vmem_shape if stay else jax.ShapeDtypeStruct)(shape, dtype) for shape, dtype in outs] + [TOKEN],
        scratch_shapes=list(scratch),
        compiler_params=pltpu.CompilerParams(vmem_limit_bytes=VMEM_BYTES),
        cost_estimate=cost(micros),
        name=name,
    )(where, *map(in_vmem, operands))
    return where, held


def per_device(tokens, cotangent, probs, experts, w_gate, w_up, w_down):
    rows, features = tokens.shape
    top = experts.shape[1]
    zs, xs = lax.axis_size("expert"), lax.axis_size("blk")
    cores = lax.axis_size("tensor")
    positions = zs * xs
    half = rows // cores
    halves, _, quarter = w_gate.shape
    span = 2 if halves % 2 == 0 else 1
    count = halves // span
    hidden = span * quarter
    slots = positions * MOST
    core = lax.axis_index("tensor")
    position = lax.axis_index("expert") * xs + lax.axis_index("blk")
    kinds = 8 * pl.cdiv(top, 8)
    barrier = lax.optimization_barrier

    def swap(array):
        return lax.ppermute(array, "tensor", [(i, (i + 1) % cores) for i in range(cores)])

    def along_z(array, by):
        return lax.ppermute(array, "expert", [(i, (i + by) % zs) for i in range(zs)])

    def along_x(array, by):
        return lax.ppermute(array, "blk", [(i, (i + by) % xs) for i in range(xs)])

    wg = jnp.swapaxes(w_gate, 1, 2).reshape(count, hidden, features)
    wu = jnp.swapaxes(w_up, 1, 2).reshape(count, hidden, features)
    wd = w_down.reshape(count, hidden, features)
    where = jnp.stack([position * halves, core]).astype(jnp.int32)
    group = zs * MOST
    packed = features // rows * half
    own_x, own_dy, where = pl.pallas_call(
        pack,
        in_specs=[SCALARS] + [pl.BlockSpec(memory_space=pl.ANY)] * 4,
        out_specs=[IN_VMEM] * 2 + [SCALARS],
        out_shape=[jax.ShapeDtypeStruct((packed + 2 * kinds, rows), BF16), jax.ShapeDtypeStruct((half, features), BF16),
                   TOKEN],
        scratch_shapes=[pltpu.VMEM((half, features), BF16), pltpu.VMEM((top, rows), jnp.int32),
                        pltpu.VMEM((top, rows), BF16), pltpu.VMEM((kinds, rows), F32), pltpu.VMEM((kinds, rows), F32),
                        pltpu.SemaphoreType.DMA((4,))],
        compiler_params=pltpu.CompilerParams(vmem_limit_bytes=VMEM_BYTES),
        cost_estimate=cost(2),
        name="pack",
    )(where, in_hbm(tokens), in_hbm(cotangent), in_hbm(experts.T), in_hbm(probs.T))

    line_x = [along_z(own_x, d) for d in range(1, zs)]
    first_x = [along_x(own_x, c) for c in range(1, xs)]
    first_dy = [along_x(own_dy, c) for c in range(1, xs)]
    where, (wg, wu, wd) = load(where, (wg, wu, wd))
    where, line_x, first_x, first_dy, own_dy = barrier((where, line_x, first_x, first_dy, own_dy))

    line_dy = [along_z(own_dy, d) for d in range(1, zs)]
    rest = jnp.stack(line_x)
    more = [along_x(rest, c) for c in range(1, xs)]
    rows_x, ranks, weight, metas = [], [], [], []

    def take_tokens(where, near, far):
        outs = [((count, group, features), BF16), ((zs * count, rows), F32), ((zs * count, rows), F32),
                ((zs, 2 * kinds, rows), F32)]
        where, results = on_vmem(functools.partial(select_tokens, span), "select_tokens", 2, outs, where, (near, far))
        for held, result in zip((rows_x, ranks, weight, metas), results):
            held.append(result)
        return where

    def take_cotangents(where, near, far):
        outs = [((count, group, features), BF16)]
        return on_vmem(select_cotangents, "select_cotangents", 2, outs, where, (ranks[len(rows_dy)], near, far))

    near = jnp.concatenate([own_x[None], rest])
    where = take_tokens(where, near, swap(near))
    where, line_dy, more = barrier((where, line_dy, more))
    groups_x = [jnp.concatenate([a[None], b]) for a, b in zip(first_x, more)]

    rest = jnp.stack(line_dy)
    more = [along_x(rest, c) for c in range(1, xs)]
    rows_dy = []
    for near in groups_x:
        where = take_tokens(where, near, swap(near))
    where, (gate, up) = on_vmem(forward_kernel, "forward", 5, [((count, hidden, slots), F32)] * 2, where, (wg, wu, *rows_x))
    near = jnp.concatenate([own_dy[None], rest])
    where, got = take_cotangents(where, near, swap(near))
    rows_dy += got
    where, more = barrier((where, more))
    for near in [jnp.concatenate([a[None], b]) for a, b in zip(first_dy, more)]:
        where, got = take_cotangents(where, near, swap(near))
        rows_dy += got

    outs = [((count, hidden, slots), BF16)] * 3 + [((count, slots, features), BF16), ((count, positions, rows), F32)]
    where, (dgate, dup, gated, rows_in, prob) = on_vmem(
        functools.partial(backward_kernel, xs), "backward", 9, outs, where,
        (wg, wu, wd, gate, up, *ranks, *weight, *rows_dy))
    height = packed + 16 * pl.cdiv(kinds, 16)
    split = 2 * height // 3 // 16 * 16
    chip = [None] * xs
    for c in list(range(1, xs)) + [0]:
        where, (own, other) = on_vmem(
            functools.partial(put_back, span, c * zs), "put_back", 2, [((zs, height, rows), BF16)] * 2, where,
            (ranks[c], metas[c], rows_in, prob), False)
        chip[c] = own, swap(other)

    def both_cores(c, index):
        own, other = chip[c]
        return own[index].astype(F32) + other[index].astype(F32)

    saved = (dgate, dup, gated, *rows_x, *rows_dy)

    def weights(where, after):
        depth = min(count, 2)
        *grads, where = pl.pallas_call(
            functools.partial(weights_kernel, xs),
            in_specs=[SCALARS] + [IN_VMEM] * len(saved) + [pl.BlockSpec(memory_space=pl.ANY)] * len(after),
            out_specs=[pl.BlockSpec(memory_space=pl.ANY)] * 3 + [SCALARS],
            out_shape=[jax.ShapeDtypeStruct((count, hidden, features), BF16)] * 3 + [TOKEN],
            scratch_shapes=[pltpu.VMEM((depth, 3, hidden, features), BF16), pltpu.SemaphoreType.DMA((depth, 3))],
            compiler_params=pltpu.CompilerParams(vmem_limit_bytes=VMEM_BYTES),
            cost_estimate=cost(9),
            name="weights",
        )(where, *map(in_vmem, saved), *after)
        return where, grads

    first, last = slice(0, split), slice(split, height)
    crossing = [both_cores(c, (slice(None), first)).astype(BF16) for c in range(1, xs)]
    sides = [jnp.stack([both_cores(c, (d, last)) for c in range(xs)]) for d in range(zs)]
    lining = [side.astype(BF16) for side in sides[1:]]
    hops = [along_x(array, -c) for c, array in enumerate(crossing, 1)]
    shifts = [along_z(array, -d) for d, array in enumerate(lining, 1)]
    where, grads = weights(where, crossing + lining)
    outs = [((split, rows), BF16 if d else F32) for d in range(zs)]
    outs += [((height - split, rows), BF16 if c else F32) for c in range(xs)]
    where, sums = on_vmem(functools.partial(middle_sums, zs, xs), "middle_sums", 1, outs, where,
                          (*chip[0], sides[0], *hops, *shifts), False)
    parts = [along_z(sums[d], -d) if d else sums[d] for d in range(zs)]
    parts += [along_x(sums[zs + c], -c) if c else sums[zs] for c in range(xs)]
    where, (mine,) = on_vmem(functools.partial(last_sums, zs, xs), "last_sums", 1, [((height, rows), BF16)], where,
                             parts, False)
    outs = [((rows, features), BF16), ((top, rows), F32)]
    where, (grad_tokens, grad_probs) = on_vmem(unpack, "unpack", 1, outs, where, (mine, swap(mine)), False)
    grad_probs = grad_probs.T
    grad_gate, grad_up, grad_down = grads
    shape = (halves, quarter, features)
    return (
        grad_tokens,
        grad_probs,
        jnp.swapaxes(grad_gate.reshape(shape), 1, 2),
        jnp.swapaxes(grad_up.reshape(shape), 1, 2),
        grad_down.reshape(shape),
    )


def solution(mesh):
    return jax.shard_map(
        per_device,
        mesh=mesh,
        in_specs=(
            P(("groups", "expert", "blk"), None),
            P(("groups", "expert", "blk"), None),
            P(("groups", "expert", "blk"), None),
            P(("groups", "expert", "blk"), None),
            P(("expert", "blk"), None, "tensor"),
            P(("expert", "blk"), None, "tensor"),
            P(("expert", "blk"), "tensor", None),
        ),
        out_specs=(
            P(("groups", "expert", "blk"), None),
            P(("groups", "expert", "blk"), None),
            P(("groups", "expert", "blk"), None, "tensor"),
            P(("groups", "expert", "blk"), None, "tensor"),
            P(("groups", "expert", "blk"), "tensor", None),
        ),
        check_vma=False,
    )
```

```python
import functools

import jax
import jax.numpy as jnp
from jax import lax
from jax.experimental import pallas as pl
from jax.experimental.pallas import tpu as pltpu
from jax.sharding import PartitionSpec as P

MOST = 16
BF16, F32 = jnp.bfloat16, jnp.float32
LAST = (((1,), (1,)), ((), ()))
LEAD = (((0,), (0,)), ((), ()))
VMEM_BYTES = 12 * 1024 * 1024


def cost(micros):
    return pl.CostEstimate(flops=1000, bytes_accessed=int(micros * 3_000_000), transcendentals=0)


def dot(a, b, dims):
    return lax.dot_general(a, b, dims, preferred_element_type=F32)


def iota(shape, dim):
    return lax.broadcasted_iota(jnp.int32, shape, dim)


def ranks_and_probs(first, meta, span, count):
    sources, height, tokens = meta.shape
    kinds = height // 2
    wanted = ((first + span * iota((count, tokens), 0)) >> 1).astype(F32)
    named, weight = [], []
    for source in range(sources):
        entry = meta[source].astype(F32)
        hit = jnp.zeros((count, tokens), F32)
        prob = jnp.zeros((count, tokens), F32)
        for kind in range(kinds):
            same = entry[kind : kind + 1] == wanted
            hit = jnp.where(same, 1.0, hit)
            prob = jnp.where(same, entry[kinds + kind : kinds + kind + 1], prob)
        named.append(hit)
        weight.append(prob)
    named = jnp.concatenate(named)
    before = (iota((tokens, tokens), 0) < iota((tokens, tokens), 1)).astype(F32).astype(BF16)
    rank = jnp.dot(named.astype(BF16), before, preferred_element_type=F32)
    return jnp.where(named > 0, rank, -1.0), jnp.concatenate(weight)


def slot_matrix(rank):
    count, tokens = rank.shape
    wide = jnp.broadcast_to(rank[:, None, :], (count, MOST, tokens)).reshape(count * MOST, tokens)
    place = (iota((count * MOST, tokens), 0) & (MOST - 1)).astype(F32)
    return jnp.where(wide == place, 1.0, 0.0).astype(BF16)


def select(rank, near, far, rows_ref):
    count, sources = rows_ref.shape[0], rows_ref.shape[1] // MOST
    for source in range(sources):
        pick = slot_matrix(rank[source * count : (source + 1) * count])
        both = jnp.concatenate([near(source), far(source)], axis=0)
        rows = jnp.dot(pick, both, preferred_element_type=F32).astype(BF16)
        rows_ref[:, source * MOST : (source + 1) * MOST, :] = rows.reshape(count, MOST, rows.shape[1])


def unpacked(piece, half, features):
    chunks = features // piece.shape[1]
    return jnp.concatenate([piece[chunk * half : (chunk + 1) * half] for chunk in range(chunks)], axis=1)


def store_packed(ref, index, rows):
    half, features = rows.shape
    lanes = ref.shape[-1]
    for chunk in range(features // lanes):
        ref[(*index, slice(chunk * half, (chunk + 1) * half))] = rows[:, chunk * lanes : (chunk + 1) * lanes]


def pack(core_ref, where_ref, tokens_ref, cotangent_ref, experts_ref, probs_ref, x_ref, dy_ref, token_ref, half_scr, experts_scr,
         chosen_scr, ids_scr, prob_scr, sems):
    second = core_ref[0] == 1
    half = dy_ref.shape[0]
    top, kinds = experts_ref.shape[0], ids_scr.shape[0]
    mine = pl.ds(pl.multiple_of(core_ref[0] * half, half), half)
    pairs = ((tokens_ref.at[mine], half_scr), (experts_ref, experts_scr), (probs_ref, chosen_scr),
             (cotangent_ref.at[mine], dy_ref))
    copies = [pltpu.make_async_copy(source, target, sems.at[at]) for at, (source, target) in enumerate(pairs)]
    for copy in copies:
        copy.start()
    pass_on(where_ref, token_ref)
    for copy in copies:
        copy.wait()
    store_packed(x_ref, (), half_scr[...])
    ids_scr[...] = jnp.full(ids_scr.shape, -1.0, F32)
    prob_scr[...] = jnp.zeros(prob_scr.shape, F32)
    ids_scr[:top] = experts_scr[...].astype(F32)
    prob_scr[:top] = chosen_scr[...].astype(F32)
    lines = [jnp.where(second, pltpu.roll(ref[...], half, 1), ref[...]) for ref in (ids_scr, prob_scr)]
    x_ref[x_ref.shape[0] - 2 * kinds :] = jnp.concatenate(lines, axis=0).astype(BF16)


def select_tokens(span, where_ref, near_ref, far_ref, rows_ref, rank_ref, weight_ref, meta_ref):
    half, features, height = rank_ref.shape[1] // 2, rows_ref.shape[2], meta_ref.shape[1]
    meta = near_ref[:, near_ref.shape[1] - height :, :].astype(F32)
    rank, weight = ranks_and_probs(where_ref[0:1, : meta.shape[2]], meta, span, rows_ref.shape[0])
    rank_ref[...] = rank
    weight_ref[...] = weight
    meta_ref[...] = meta
    select(rank, lambda source: unpacked(near_ref[source], half, features),
           lambda source: unpacked(far_ref[source], half, features), rows_ref)


def select_cotangents(where_ref, rank_ref, near_ref, far_ref, rows_ref):
    select(rank_ref[...], lambda source: near_ref[source], lambda source: far_ref[source], rows_ref)


def joined(refs, index):
    return jnp.concatenate([ref[index] for ref in refs], axis=0)


def each(count, body):
    def step(index, carry):
        body(index)
        return carry

    lax.fori_loop(0, count, step, 0, unroll=8 if count % 8 == 0 else 1)


def forward_kernel(where_ref, wg_ref, wu_ref, *refs):
    rows_refs, (gate_ref, up_ref) = refs[:-2], refs[-2:]

    def body(expert):
        rows = joined(rows_refs, expert)
        gate_ref[expert] = dot(wg_ref[expert], rows, LAST)
        up_ref[expert] = dot(wu_ref[expert], rows, LAST)

    each(gate_ref.shape[0], body)


def backward_kernel(groups, where_ref, wg_ref, wu_ref, wd_ref, gate_ref, up_ref, *refs):
    rank_refs, weight_refs, rows_refs = refs[:groups], refs[groups : 2 * groups], refs[2 * groups : 3 * groups]
    dgate_ref, dup_ref, gated_ref, input_ref, prob_ref = refs[3 * groups :]
    count, slots, _ = input_ref.shape
    sources, tokens = prob_ref.shape[1:]
    total = sources * count
    rank = joined(rank_refs, ...).astype(BF16)
    weight = joined(weight_refs, ...).astype(BF16)
    place = (iota((tokens, slots), 1) & (MOST - 1)).astype(F32)
    row, lane = iota((total, slots), 0), iota((total, slots), 1)
    block = jnp.where(iota((sources, slots), 0) == iota((sources, slots), 1) // MOST, 1.0, 0.0).astype(BF16)

    def body(expert):
        spread = jnp.where(row == (lane // MOST) * count + expert, 1.0, 0.0).astype(BF16)
        holds = dot(rank, spread, LEAD) == place
        scale = jnp.sum(jnp.where(holds, dot(weight, spread, LEAD), 0.0), axis=0, keepdims=True)
        raw = dot(wd_ref[expert], joined(rows_refs, expert), LAST)
        gate, up = gate_ref[expert], up_ref[expert]
        sigmoid = 1.0 / (1.0 + jnp.exp(-gate))
        active = gate * sigmoid
        hidden = active * up
        gated_ref[expert] = (scale * hidden).astype(BF16)
        prob = jnp.sum(hidden * raw, axis=0, keepdims=True)
        scaled = scale * raw
        dgate = (scaled * up * sigmoid * (1.0 + gate * (1.0 - sigmoid))).astype(BF16)
        dup = (scaled * active).astype(BF16)
        dgate_ref[expert] = dgate
        dup_ref[expert] = dup
        input_ref[expert] = (dot(dgate, wg_ref[expert], LEAD) + dot(dup, wu_ref[expert], LEAD)).astype(BF16)
        prob_ref[expert] = dot(block, jnp.where(holds, prob, 0.0).astype(BF16), LAST)

    each(count, body)


def put_back(span, base, where_ref, rank_ref, meta_ref, input_ref, prob_ref, own_ref, other_ref):
    count, _, features = input_ref.shape
    tokens = rank_ref.shape[1]
    half, kinds = tokens // 2, meta_ref.shape[1] // 2
    tail = own_ref.shape[1] - features // own_ref.shape[2] * half
    wanted = ((where_ref[0:1, :tokens] + span * iota((count, tokens), 0)) >> 1).astype(F32)
    for source in range(own_ref.shape[0]):
        number = base + source
        pick = slot_matrix(rank_ref[source * count : (source + 1) * count])
        rows = input_ref[:, number * MOST : (number + 1) * MOST, :].reshape(count * MOST, features)
        part = dot(pick, rows, LEAD).astype(BF16)
        store_packed(own_ref, (source,), part[:half])
        store_packed(other_ref, (source,), part[half:])
        prob = prob_ref[:, number, :]
        entry = meta_ref[source]
        lines = jnp.zeros((tail, tokens), F32)
        for kind in range(kinds):
            line = jnp.sum(jnp.where(entry[kind : kind + 1] == wanted, prob, 0.0), axis=0, keepdims=True)
            lines = jnp.where(iota((tail, tokens), 0) == kind, line, lines)
        own_ref[source, own_ref.shape[1] - tail :] = lines.astype(BF16)
        other_ref[source, own_ref.shape[1] - tail :] = pltpu.roll(lines, half, 1).astype(BF16)


def weights_kernel(groups, number, where_ref, *refs):
    hidden_refs, rows_refs = refs[:number], refs[number : number + groups]
    targets, token_ref, slots_ref, sems = refs[-3 - number : -3], *refs[-3:]
    count, depth = hidden_refs[0].shape[0], slots_ref.shape[0]

    def copies(expert):
        slot = lax.rem(expert, depth)
        return [
            pltpu.make_async_copy(slots_ref.at[slot, at], target.at[expert], sems.at[slot, at])
            for at, target in enumerate(targets)
        ]

    def body(expert, carry):
        @pl.when(expert >= depth)
        def _():
            for copy in copies(expert - depth):
                copy.wait()

        slot = lax.rem(expert, depth)
        rows = joined(rows_refs, expert)
        for at, hidden_ref in enumerate(hidden_refs):
            slots_ref[slot, at] = jnp.dot(hidden_ref[expert], rows, preferred_element_type=F32).astype(BF16)
        for copy in copies(expert):
            copy.start()
        return carry

    lax.fori_loop(0, count, body, 0)
    for expert in range(max(count - depth, 0), count):
        for copy in copies(expert):
            copy.wait()
    pass_on(where_ref, token_ref)


def middle_sums(zs, xs, where_ref, own_ref, other_ref, base_ref, *refs):
    hops, shifts, outs = refs[: xs - 1], refs[xs - 1 : xs + zs - 2], refs[xs + zs - 2 :]
    size = hops[0].shape[1]
    for place in range(zs):
        total = own_ref[place, :size].astype(F32) + other_ref[place, :size].astype(F32)
        for hop in hops:
            total = total + hop[place].astype(F32)
        outs[place][...] = total.astype(outs[place].dtype)
    for place in range(xs):
        total = base_ref[place]
        for piece in shifts:
            total = total + piece[place].astype(F32)
        outs[zs + place][...] = total.astype(outs[zs + place].dtype)


def last_sums(zs, xs, where_ref, *refs):
    first, last, out = refs[:zs], refs[zs : zs + xs], refs[-1]
    size = first[0].shape[0]
    for refs, rows in ((first, slice(0, size)), (last, slice(size, out.shape[0]))):
        total = refs[0][...]
        for ref in refs[1:]:
            total = total + ref[...].astype(F32)
        out[rows] = total.astype(BF16)


def unpack(where_ref, mine_ref, theirs_ref, tokens_ref, probs_ref):
    mine, theirs = mine_ref[...].astype(F32), theirs_ref[...].astype(F32)
    second = jnp.broadcast_to(where_ref[1:2, : mine.shape[1]], mine.shape) == 1
    half, features = tokens_ref.shape[0] // 2, tokens_ref.shape[1]
    low, high = jnp.where(second, theirs, mine), jnp.where(second, mine, theirs)
    tokens_ref[:half] = unpacked(low, half, features).astype(BF16)
    tokens_ref[half:] = unpacked(high, half, features).astype(BF16)
    at = features // low.shape[1] * half
    low, high = low[at:], high[at:]
    both = jnp.where(iota(low.shape, 1) < half, low, pltpu.roll(high, half, 1))
    probs_ref[...] = both[: probs_ref.shape[0]]


def in_vmem(array):
    return pltpu.with_memory_space_constraint(array, pltpu.VMEM)


def in_hbm(array):
    return pltpu.with_memory_space_constraint(array, pltpu.HBM)


def vmem_shape(shape, dtype):
    return pltpu.VMEM(shape, dtype)


def in_hbm(array):
    return pltpu.with_memory_space_constraint(array, pltpu.HBM)


def vmem_shape(shape, dtype):
    return pltpu.VMEM(shape, dtype)


def pass_on(where_ref, token_ref):
    token_ref[...] = where_ref[...]


def load_kernel(where_ref, *refs):
    count = (len(refs) - 2) // 2
    token_ref, sems = refs[2 * count :]
    copies = [
        pltpu.make_async_copy(source, target, sems.at[number])
        for number, (source, target) in enumerate(zip(refs[:count], refs[count : 2 * count]))
    ]
    for copy in copies:
        copy.start()
    for copy in copies:
        copy.wait()
    pass_on(where_ref, token_ref)


SCALARS = pl.BlockSpec(memory_space=pltpu.SMEM)
IN_VMEM = pl.BlockSpec(memory_space=pltpu.VMEM)
WHERE = (8, 128)


def load(where, arrays):
    *held, where = pl.pallas_call(
        load_kernel,
        in_specs=[IN_VMEM] + [pl.BlockSpec(memory_space=pl.ANY)] * len(arrays),
        out_specs=[IN_VMEM] * len(arrays) + [IN_VMEM],
        out_shape=[vmem_shape(array.shape, array.dtype) for array in arrays] + [vmem_shape(WHERE, jnp.int32)],
        scratch_shapes=[pltpu.SemaphoreType.DMA((len(arrays),))],
        compiler_params=pltpu.CompilerParams(vmem_limit_bytes=VMEM_BYTES),
        cost_estimate=cost(7),
        name="load",
    )(in_vmem(where), *map(in_hbm, arrays))
    return where, held


def on_vmem(kernel, name, micros, outs, where, operands, stay=True, scratch=()):
    def body(where_ref, *refs):
        at = len(operands) + len(outs)
        kernel(where_ref, *refs[:at], *refs[at + 1 :])
        pass_on(where_ref, refs[at])

    *held, where = pl.pallas_call(
        body,
        in_specs=[IN_VMEM] * (1 + len(operands)),
        out_specs=[IN_VMEM] * (len(outs) + 1),
        out_shape=[(vmem_shape if stay else jax.ShapeDtypeStruct)(shape, dtype) for shape, dtype in outs] + [vmem_shape(WHERE, jnp.int32)],
        scratch_shapes=list(scratch),
        compiler_params=pltpu.CompilerParams(vmem_limit_bytes=VMEM_BYTES),
        cost_estimate=cost(micros),
        name=name,
    )(in_vmem(where), *map(in_vmem, operands))
    return where, held


def per_device(tokens, cotangent, probs, experts, w_gate, w_up, w_down):
    rows, features = tokens.shape
    top = experts.shape[1]
    zs, xs = lax.axis_size("expert"), lax.axis_size("blk")
    cores = lax.axis_size("tensor")
    positions = zs * xs
    half = rows // cores
    halves, _, quarter = w_gate.shape
    span = 2 if halves % 2 == 0 else 1
    count = halves // span
    hidden = span * quarter
    slots = positions * MOST
    core = lax.axis_index("tensor")
    position = lax.axis_index("expert") * xs + lax.axis_index("blk")
    kinds = 8 * pl.cdiv(top, 8)
    barrier = lax.optimization_barrier

    def swap(array):
        return lax.ppermute(array, "tensor", [(i, (i + 1) % cores) for i in range(cores)])

    def along_z(array, by):
        return lax.ppermute(array, "expert", [(i, (i + by) % zs) for i in range(zs)])

    def along_x(array, by):
        return lax.ppermute(array, "blk", [(i, (i + by) % xs) for i in range(xs)])

    wg = jnp.swapaxes(w_gate, 1, 2).reshape(count, hidden, features)
    wu = jnp.swapaxes(w_up, 1, 2).reshape(count, hidden, features)
    wd = w_down.reshape(count, hidden, features)
    where = jnp.where(iota(WHERE, 0) == 0, position * halves, core).astype(jnp.int32)
    group = zs * MOST
    packed = features // rows * half
    own_x, own_dy, where = pl.pallas_call(
        pack,
        in_specs=[SCALARS, IN_VMEM] + [pl.BlockSpec(memory_space=pl.ANY)] * 4,
        out_specs=[IN_VMEM] * 3,
        out_shape=[jax.ShapeDtypeStruct((packed + 2 * kinds, rows), BF16), jax.ShapeDtypeStruct((half, features), BF16),
                   vmem_shape(WHERE, jnp.int32)],
        scratch_shapes=[pltpu.VMEM((half, features), BF16), pltpu.VMEM((top, rows), jnp.int32),
                        pltpu.VMEM((top, rows), BF16), pltpu.VMEM((kinds, rows), F32), pltpu.VMEM((kinds, rows), F32),
                        pltpu.SemaphoreType.DMA((4,))],
        compiler_params=pltpu.CompilerParams(vmem_limit_bytes=VMEM_BYTES),
        cost_estimate=cost(2),
        name="pack",
    )(core.astype(jnp.int32).reshape(1), in_vmem(where), in_hbm(tokens), in_hbm(cotangent), in_hbm(experts.T), in_hbm(probs.T))

    line_x = [along_z(own_x, d) for d in range(1, zs)]
    first_x = [along_x(own_x, c) for c in range(1, xs)]
    first_dy = [along_x(own_dy, c) for c in range(1, xs)]
    where, (wg, wu, wd) = load(where, (wg, wu, wd))
    where, line_x, first_x, first_dy, own_dy = barrier((where, line_x, first_x, first_dy, own_dy))

    line_dy = [along_z(own_dy, d) for d in range(1, zs)]
    rest = jnp.stack(line_x)
    more = [along_x(rest, c) for c in range(1, xs)]
    rows_x, ranks, weight, metas = [], [], [], []

    def take_tokens(where, near, far):
        outs = [((count, group, features), BF16), ((zs * count, rows), F32), ((zs * count, rows), F32),
                ((zs, 2 * kinds, rows), F32)]
        where, results = on_vmem(functools.partial(select_tokens, span), "select_tokens", 2, outs, where, (near, far))
        for held, result in zip((rows_x, ranks, weight, metas), results):
            held.append(result)
        return where

    def take_cotangents(where, near, far):
        outs = [((count, group, features), BF16)]
        return on_vmem(select_cotangents, "select_cotangents", 2, outs, where, (ranks[len(rows_dy)], near, far))

    near = jnp.concatenate([own_x[None], rest])
    where = take_tokens(where, near, swap(near))
    where, line_dy, more = barrier((where, line_dy, more))
    groups_x = [jnp.concatenate([a[None], b]) for a, b in zip(first_x, more)]

    rest = jnp.stack(line_dy)
    more = [along_x(rest, c) for c in range(1, xs)]
    rows_dy = []
    for near in groups_x:
        where = take_tokens(where, near, swap(near))
    where, (gate, up) = on_vmem(forward_kernel, "forward", 5, [((count, hidden, slots), F32)] * 2, where, (wg, wu, *rows_x))
    near = jnp.concatenate([own_dy[None], rest])
    where, got = take_cotangents(where, near, swap(near))
    rows_dy += got
    where, more = barrier((where, more))
    for near in [jnp.concatenate([a[None], b]) for a, b in zip(first_dy, more)]:
        where, got = take_cotangents(where, near, swap(near))
        rows_dy += got

    outs = [((count, hidden, slots), BF16)] * 3 + [((count, slots, features), BF16), ((count, positions, rows), F32)]
    where, (dgate, dup, gated, rows_in, prob) = on_vmem(
        functools.partial(backward_kernel, xs), "backward", 9, outs, where,
        (wg, wu, wd, gate, up, *ranks, *weight, *rows_dy))
    height = packed + 16 * pl.cdiv(kinds, 16)
    split = 2 * height // 3 // 16 * 16
    chip = [None] * xs
    for c in list(range(1, xs)) + [0]:
        where, (own, other) = on_vmem(
            functools.partial(put_back, span, c * zs), "put_back", 2, [((zs, height, rows), BF16)] * 2, where,
            (ranks[c], metas[c], rows_in, prob), False)
        chip[c] = own, swap(other)

    def both_cores(c, index):
        own, other = chip[c]
        return own[index].astype(F32) + other[index].astype(F32)

    def weights(where, sources, shared, after):
        depth, number = min(count, 3), len(sources)
        operands = [in_vmem(array) for array in (*sources, *shared)]
        *grads, where = pl.pallas_call(
            functools.partial(weights_kernel, xs, number),
            in_specs=[IN_VMEM] * (1 + len(operands)) + [pl.BlockSpec(memory_space=pl.ANY)] * len(after),
            out_specs=[pl.BlockSpec(memory_space=pl.ANY)] * number + [IN_VMEM],
            out_shape=[jax.ShapeDtypeStruct((count, hidden, features), BF16)] * number + [vmem_shape(WHERE, jnp.int32)],
            scratch_shapes=[pltpu.VMEM((depth, number, hidden, features), BF16), pltpu.SemaphoreType.DMA((depth, number))],
            compiler_params=pltpu.CompilerParams(vmem_limit_bytes=VMEM_BYTES),
            cost_estimate=cost(3 * number),
            name="weights",
        )(in_vmem(where), *operands, *after)
        return where, grads

    first, last = slice(0, split), slice(split, height)
    crossing = [both_cores(c, (slice(None), first)).astype(BF16) for c in range(1, xs)]
    sides = [jnp.stack([both_cores(c, (d, last)) for c in range(xs)]) for d in range(zs)]
    lining = [side.astype(BF16) for side in sides[1:]]
    hops = [along_x(array, -c) for c, array in enumerate(crossing, 1)]
    shifts = [along_z(array, -d) for d, array in enumerate(lining, 1)]
    where, (grad_gate, grad_up) = weights(where, (dgate, dup), rows_x, crossing + lining)
    outs = [((split, rows), BF16 if d else F32) for d in range(zs)]
    outs += [((height - split, rows), BF16 if c else F32) for c in range(xs)]
    where, sums = on_vmem(functools.partial(middle_sums, zs, xs), "middle_sums", 1, outs, where,
                          (*chip[0], sides[0], *hops, *shifts), False)
    parts = [along_z(sums[d], -d) if d else sums[d] for d in range(zs)]
    parts += [along_x(sums[zs + c], -c) if c else sums[zs] for c in range(xs)]
    where, (grad_down,) = weights(where, (gated,), rows_dy, [array for array in sums if array.dtype == BF16])
    where, (mine,) = on_vmem(functools.partial(last_sums, zs, xs), "last_sums", 1, [((height, rows), BF16)], where,
                             parts, False)
    outs = [((rows, features), BF16), ((top, rows), F32)]
    where, (grad_tokens, grad_probs) = on_vmem(unpack, "unpack", 1, outs, where, (mine, swap(mine)), False)
    grad_probs = grad_probs.T
    shape = (halves, quarter, features)
    return (
        grad_tokens,
        grad_probs,
        jnp.swapaxes(grad_gate.reshape(shape), 1, 2),
        jnp.swapaxes(grad_up.reshape(shape), 1, 2),
        grad_down.reshape(shape),
    )


def solution(mesh):
    return jax.shard_map(
        per_device,
        mesh=mesh,
        in_specs=(
            P(("groups", "expert", "blk"), None),
            P(("groups", "expert", "blk"), None),
            P(("groups", "expert", "blk"), None),
            P(("groups", "expert", "blk"), None),
            P(("expert", "blk"), None, "tensor"),
            P(("expert", "blk"), None, "tensor"),
            P(("expert", "blk"), "tensor", None),
        ),
        out_specs=(
            P(("groups", "expert", "blk"), None),
            P(("groups", "expert", "blk"), None),
            P(("groups", "expert", "blk"), None, "tensor"),
            P(("groups", "expert", "blk"), None, "tensor"),
            P(("groups", "expert", "blk"), "tensor", None),
        ),
        check_vma=False,
    )
```

```python
import functools

import jax
import jax.numpy as jnp
from jax import lax
from jax.experimental import pallas as pl
from jax.experimental.pallas import tpu as pltpu
from jax.sharding import PartitionSpec as P

MOST = 16
BF16, F32 = jnp.bfloat16, jnp.float32
LAST = (((1,), (1,)), ((), ()))
LEAD = (((0,), (0,)), ((), ()))
VMEM_BYTES = 12 * 1024 * 1024


def cost(micros):
    return pl.CostEstimate(flops=1000, bytes_accessed=int(micros * 3_000_000), transcendentals=0)


def dot(a, b, dims):
    return lax.dot_general(a, b, dims, preferred_element_type=F32)


def iota(shape, dim):
    return lax.broadcasted_iota(jnp.int32, shape, dim)


def ranks_and_probs(first, meta, span, count):
    sources, height, tokens = meta.shape
    kinds = height // 2
    wanted = ((first + span * iota((count, tokens), 0)) >> 1).astype(F32)
    named, weight = [], []
    for source in range(sources):
        entry = meta[source].astype(F32)
        hit = jnp.zeros((count, tokens), F32)
        prob = jnp.zeros((count, tokens), F32)
        for kind in range(kinds):
            same = entry[kind : kind + 1] == wanted
            hit = jnp.where(same, 1.0, hit)
            prob = jnp.where(same, entry[kinds + kind : kinds + kind + 1], prob)
        named.append(hit)
        weight.append(prob)
    named = jnp.concatenate(named)
    before = (iota((tokens, tokens), 0) < iota((tokens, tokens), 1)).astype(F32).astype(BF16)
    rank = jnp.dot(named.astype(BF16), before, preferred_element_type=F32)
    return jnp.where(named > 0, rank, -1.0), jnp.concatenate(weight)


def slot_matrix(rank):
    count, tokens = rank.shape
    wide = jnp.broadcast_to(rank[:, None, :], (count, MOST, tokens)).reshape(count * MOST, tokens)
    place = (iota((count * MOST, tokens), 0) & (MOST - 1)).astype(F32)
    return jnp.where(wide == place, 1.0, 0.0).astype(BF16)


def select(rank, near, far, rows_ref):
    count, sources = rows_ref.shape[0], rows_ref.shape[1] // MOST
    for source in range(sources):
        pick = slot_matrix(rank[source * count : (source + 1) * count])
        both = jnp.concatenate([near(source), far(source)], axis=0)
        rows = jnp.dot(pick, both, preferred_element_type=F32).astype(BF16)
        rows_ref[:, source * MOST : (source + 1) * MOST, :] = rows.reshape(count, MOST, rows.shape[1])


def unpacked(piece, half, features):
    chunks = features // piece.shape[1]
    return jnp.concatenate([piece[chunk * half : (chunk + 1) * half] for chunk in range(chunks)], axis=1)


def store_packed(ref, index, rows):
    half, features = rows.shape
    lanes = ref.shape[-1]
    for chunk in range(features // lanes):
        ref[(*index, slice(chunk * half, (chunk + 1) * half))] = rows[:, chunk * lanes : (chunk + 1) * lanes]


def pack(core_ref, where_ref, tokens_ref, cotangent_ref, experts_ref, probs_ref, x_ref, dy_ref, token_ref, half_scr, experts_scr,
         chosen_scr, ids_scr, prob_scr, sems):
    second = core_ref[0] == 1
    half = dy_ref.shape[0]
    top, kinds = experts_ref.shape[0], ids_scr.shape[0]
    mine = pl.ds(pl.multiple_of(core_ref[0] * half, half), half)
    pairs = ((tokens_ref.at[mine], half_scr), (experts_ref, experts_scr), (probs_ref, chosen_scr),
             (cotangent_ref.at[mine], dy_ref))
    copies = [pltpu.make_async_copy(source, target, sems.at[at]) for at, (source, target) in enumerate(pairs)]
    for copy in copies:
        copy.start()
    pass_on(where_ref, token_ref)
    for copy in copies:
        copy.wait()
    store_packed(x_ref, (), half_scr[...])
    ids_scr[...] = jnp.full(ids_scr.shape, -1.0, F32)
    prob_scr[...] = jnp.zeros(prob_scr.shape, F32)
    ids_scr[:top] = experts_scr[...].astype(F32)
    prob_scr[:top] = chosen_scr[...].astype(F32)
    lines = [jnp.where(second, pltpu.roll(ref[...], half, 1), ref[...]) for ref in (ids_scr, prob_scr)]
    x_ref[x_ref.shape[0] - 2 * kinds :] = jnp.concatenate(lines, axis=0).astype(BF16)


def select_tokens(span, where_ref, near_ref, far_ref, rows_ref, rank_ref, weight_ref, meta_ref):
    half, features, height = rank_ref.shape[1] // 2, rows_ref.shape[2], meta_ref.shape[1]
    meta = near_ref[:, near_ref.shape[1] - height :, :].astype(F32)
    rank, weight = ranks_and_probs(where_ref[0:1, : meta.shape[2]], meta, span, rows_ref.shape[0])
    rank_ref[...] = rank
    weight_ref[...] = weight
    meta_ref[...] = meta
    select(rank, lambda source: unpacked(near_ref[source], half, features),
           lambda source: unpacked(far_ref[source], half, features), rows_ref)


def select_cotangents(c, where_ref, rank_ref, near_ref, far_ref, near_tail, far_tail, rows_ref):
    whole = lambda first, tail: lambda source: jnp.concatenate([first[source], tail[source, c]], axis=0)
    select(rank_ref[...], whole(near_ref, near_tail), whole(far_ref, far_tail), rows_ref)


def joined(refs, index):
    return jnp.concatenate([ref[index] for ref in refs], axis=0)


def each(count, body):
    def step(index, carry):
        body(index)
        return carry

    lax.fori_loop(0, count, step, 0, unroll=8 if count % 8 == 0 else 1)


def forward_kernel(groups, where_ref, both_ref, *refs):
    rank_refs, weight_refs, rows_refs = refs[:groups], refs[groups : 2 * groups], refs[2 * groups : 3 * groups]
    hidden_ref, fgate_ref, fup_ref, gated_ref, holds_ref = refs[3 * groups :]
    count, tokens, slots = holds_ref.shape
    rank = joined(rank_refs, ...).astype(BF16)
    weight = joined(weight_refs, ...).astype(BF16)
    place = (iota((tokens, slots), 1) & (MOST - 1)).astype(F32)
    row, lane = iota((rank.shape[0], slots), 0), iota((rank.shape[0], slots), 1)

    def body(expert):
        spread = jnp.where(row == (lane // MOST) * count + expert, 1.0, 0.0).astype(BF16)
        holds = dot(rank, spread, LEAD) == place
        scale = jnp.sum(jnp.where(holds, dot(weight, spread, LEAD), 0.0), axis=0, keepdims=True)
        holds_ref[expert] = jnp.where(holds, 1.0, 0.0).astype(BF16)
        rows = joined(rows_refs, expert)
        both = dot(both_ref[expert], rows, LAST)
        gate, up = both[: both.shape[0] // 2], both[both.shape[0] // 2 :]
        sigmoid = 1.0 / (1.0 + jnp.exp(-gate))
        active = gate * sigmoid
        hidden = active * up
        hidden_ref[expert] = hidden
        gated_ref[expert] = (scale * hidden).astype(BF16)
        fgate_ref[expert] = scale * up * sigmoid * (1.0 + gate * (1.0 - sigmoid))
        fup_ref[expert] = scale * active

    each(count, body)


def backward_kernel(groups, where_ref, both_ref, wd_ref, hidden_ref, fgate_ref, fup_ref, holds_ref, *refs):
    rows_refs, (dboth_ref, input_ref, prob_ref) = refs[:groups], refs[groups:]
    count, slots, _ = input_ref.shape
    sources = prob_ref.shape[1]
    block = jnp.where(iota((sources, slots), 0) == iota((sources, slots), 1) // MOST, 1.0, 0.0).astype(BF16)

    def body(expert):
        raw = dot(wd_ref[expert], joined(rows_refs, expert), LAST)
        dgate = (raw * fgate_ref[expert]).astype(BF16)
        dup = (raw * fup_ref[expert]).astype(BF16)
        dboth = jnp.concatenate([dgate, dup], axis=0)
        dboth_ref[expert] = dboth
        input_ref[expert] = dot(dboth, both_ref[expert], LEAD).astype(BF16)
        prob = jnp.sum(hidden_ref[expert] * raw, axis=0, keepdims=True)
        prob_ref[expert] = dot(block, (holds_ref[expert].astype(F32) * prob).astype(BF16), LAST)

    each(count, body)


def put_back(span, base, where_ref, rank_ref, meta_ref, input_ref, prob_ref, own_ref, other_ref):
    count, _, features = input_ref.shape
    tokens = rank_ref.shape[1]
    half, kinds = tokens // 2, meta_ref.shape[1] // 2
    tail = own_ref.shape[1] - features // own_ref.shape[2] * half
    wanted = ((where_ref[0:1, :tokens] + span * iota((count, tokens), 0)) >> 1).astype(F32)
    for source in range(own_ref.shape[0]):
        number = base + source
        pick = slot_matrix(rank_ref[source * count : (source + 1) * count])
        rows = input_ref[:, number * MOST : (number + 1) * MOST, :].reshape(count * MOST, features)
        part = dot(pick, rows, LEAD).astype(BF16)
        store_packed(own_ref, (source,), part[:half])
        store_packed(other_ref, (source,), part[half:])
        prob = prob_ref[:, number, :]
        entry = meta_ref[source]
        lines = jnp.zeros((tail, tokens), F32)
        for kind in range(kinds):
            line = jnp.sum(jnp.where(entry[kind : kind + 1] == wanted, prob, 0.0), axis=0, keepdims=True)
            lines = jnp.where(iota((tail, tokens), 0) == kind, line, lines)
        own_ref[source, own_ref.shape[1] - tail :] = lines.astype(BF16)
        other_ref[source, own_ref.shape[1] - tail :] = pltpu.roll(lines, half, 1).astype(BF16)


def weights_kernel(groups, number, where_ref, hidden_ref, *refs):
    rows_refs = refs[:groups]
    targets, token_ref, slots_ref, sems = refs[-3 - number : -3], *refs[-3:]
    count, depth, height = hidden_ref.shape[0], slots_ref.shape[0], hidden_ref.shape[1] // number

    def copies(expert):
        slot = lax.rem(expert, depth)
        return [
            pltpu.make_async_copy(slots_ref.at[slot, pl.ds(at * height, height)], target.at[expert], sems.at[slot, at])
            for at, target in enumerate(targets)
        ]

    def body(expert, carry):
        @pl.when(expert >= depth)
        def _():
            for copy in copies(expert - depth):
                copy.wait()

        grads = jnp.dot(hidden_ref[expert], joined(rows_refs, expert), preferred_element_type=F32)
        slots_ref[lax.rem(expert, depth)] = grads.astype(BF16)
        for copy in copies(expert):
            copy.start()
        return carry

    lax.fori_loop(0, count, body, 0)
    for expert in range(max(count - depth, 0), count):
        for copy in copies(expert):
            copy.wait()
    pass_on(where_ref, token_ref)


def middle_sums(zs, xs, where_ref, own_ref, other_ref, base_ref, *refs):
    hops, shifts, outs = refs[: xs - 1], refs[xs - 1 : xs + zs - 2], refs[xs + zs - 2 :]
    size = hops[0].shape[1]
    for place in range(zs):
        total = own_ref[place, :size].astype(F32) + other_ref[place, :size].astype(F32)
        for hop in hops:
            total = total + hop[place].astype(F32)
        outs[place][...] = total.astype(outs[place].dtype)
    for place in range(xs):
        total = base_ref[place]
        for piece in shifts:
            total = total + piece[place].astype(F32)
        outs[zs + place][...] = total.astype(outs[zs + place].dtype)


def last_sums(zs, xs, where_ref, *refs):
    first, last, out = refs[:zs], refs[zs : zs + xs], refs[-1]
    size = first[0].shape[0]
    for refs, rows in ((first, slice(0, size)), (last, slice(size, out.shape[0]))):
        total = refs[0][...]
        for ref in refs[1:]:
            total = total + ref[...].astype(F32)
        out[rows] = total.astype(BF16)


def unpack(where_ref, mine_ref, theirs_ref, tokens_ref, probs_ref):
    mine, theirs = mine_ref[...].astype(F32), theirs_ref[...].astype(F32)
    second = jnp.broadcast_to(where_ref[1:2, : mine.shape[1]], mine.shape) == 1
    half, features = tokens_ref.shape[0] // 2, tokens_ref.shape[1]
    low, high = jnp.where(second, theirs, mine), jnp.where(second, mine, theirs)
    tokens_ref[:half] = unpacked(low, half, features).astype(BF16)
    tokens_ref[half:] = unpacked(high, half, features).astype(BF16)
    at = features // low.shape[1] * half
    low, high = low[at:], high[at:]
    both = jnp.where(iota(low.shape, 1) < half, low, pltpu.roll(high, half, 1))
    probs_ref[...] = both[: probs_ref.shape[0]]


def in_vmem(array):
    return pltpu.with_memory_space_constraint(array, pltpu.VMEM)


def in_hbm(array):
    return pltpu.with_memory_space_constraint(array, pltpu.HBM)


def vmem_shape(shape, dtype):
    return pltpu.VMEM(shape, dtype)


def in_hbm(array):
    return pltpu.with_memory_space_constraint(array, pltpu.HBM)


def vmem_shape(shape, dtype):
    return pltpu.VMEM(shape, dtype)


def pass_on(where_ref, token_ref):
    token_ref[...] = where_ref[...]


def load_kernel(where_ref, gate_ref, up_ref, down_ref, both_ref, down_held, token_ref, sems):
    hidden = gate_ref.shape[1]
    pairs = ((gate_ref, both_ref.at[:, :hidden]), (up_ref, both_ref.at[:, hidden:]), (down_ref, down_held))
    copies = [pltpu.make_async_copy(source, target, sems.at[at]) for at, (source, target) in enumerate(pairs)]
    for copy in copies:
        copy.start()
    pass_on(where_ref, token_ref)
    for copy in copies:
        copy.wait()


SCALARS = pl.BlockSpec(memory_space=pltpu.SMEM)
IN_VMEM = pl.BlockSpec(memory_space=pltpu.VMEM)
WHERE = (8, 128)


def load(where, gate, up, down):
    count, hidden, features = gate.shape
    both, down, where = pl.pallas_call(
        load_kernel,
        in_specs=[IN_VMEM] + [pl.BlockSpec(memory_space=pl.ANY)] * 3,
        out_specs=[IN_VMEM] * 3,
        out_shape=[vmem_shape((count, 2 * hidden, features), gate.dtype), vmem_shape(down.shape, down.dtype),
                   vmem_shape(WHERE, jnp.int32)],
        scratch_shapes=[pltpu.SemaphoreType.DMA((3,))],
        compiler_params=pltpu.CompilerParams(vmem_limit_bytes=VMEM_BYTES),
        cost_estimate=cost(7),
        name="load",
    )(in_vmem(where), in_hbm(gate), in_hbm(up), in_hbm(down))
    return where, both, down


def on_vmem(kernel, name, micros, outs, where, operands, stay=True, scratch=()):
    def body(where_ref, *refs):
        at = len(operands) + len(outs)
        kernel(where_ref, *refs[:at], *refs[at + 1 :])
        pass_on(where_ref, refs[at])

    *held, where = pl.pallas_call(
        body,
        in_specs=[IN_VMEM] * (1 + len(operands)),
        out_specs=[IN_VMEM] * (len(outs) + 1),
        out_shape=[(vmem_shape if stay else jax.ShapeDtypeStruct)(shape, dtype) for shape, dtype in outs] + [vmem_shape(WHERE, jnp.int32)],
        scratch_shapes=list(scratch),
        compiler_params=pltpu.CompilerParams(vmem_limit_bytes=VMEM_BYTES),
        cost_estimate=cost(micros),
        name=name,
    )(in_vmem(where), *map(in_vmem, operands))
    return where, held


def per_device(tokens, cotangent, probs, experts, w_gate, w_up, w_down):
    rows, features = tokens.shape
    top = experts.shape[1]
    zs, xs = lax.axis_size("expert"), lax.axis_size("blk")
    cores = lax.axis_size("tensor")
    positions = zs * xs
    half = rows // cores
    halves, _, quarter = w_gate.shape
    span = 2 if halves % 2 == 0 else 1
    count = halves // span
    hidden = span * quarter
    slots = positions * MOST
    core = lax.axis_index("tensor")
    position = lax.axis_index("expert") * xs + lax.axis_index("blk")
    kinds = 8 * pl.cdiv(top, 8)
    barrier = lax.optimization_barrier

    def swap(array):
        return lax.ppermute(array, "tensor", [(i, (i + 1) % cores) for i in range(cores)])

    def along_z(array, by):
        return lax.ppermute(array, "expert", [(i, (i + by) % zs) for i in range(zs)])

    def along_x(array, by):
        return lax.ppermute(array, "blk", [(i, (i + by) % xs) for i in range(xs)])

    wg = jnp.swapaxes(w_gate, 1, 2).reshape(count, hidden, features)
    wu = jnp.swapaxes(w_up, 1, 2).reshape(count, hidden, features)
    wd = w_down.reshape(count, hidden, features)
    where = jnp.where(iota(WHERE, 0) == 0, position * halves, core).astype(jnp.int32)
    group = zs * MOST
    packed = features // rows * half
    own_x, own_dy, where = pl.pallas_call(
        pack,
        in_specs=[SCALARS, IN_VMEM] + [pl.BlockSpec(memory_space=pl.ANY)] * 4,
        out_specs=[IN_VMEM] * 3,
        out_shape=[jax.ShapeDtypeStruct((packed + 2 * kinds, rows), BF16), jax.ShapeDtypeStruct((half, features), BF16),
                   vmem_shape(WHERE, jnp.int32)],
        scratch_shapes=[pltpu.VMEM((half, features), BF16), pltpu.VMEM((top, rows), jnp.int32),
                        pltpu.VMEM((top, rows), BF16), pltpu.VMEM((kinds, rows), F32), pltpu.VMEM((kinds, rows), F32),
                        pltpu.SemaphoreType.DMA((4,))],
        compiler_params=pltpu.CompilerParams(vmem_limit_bytes=VMEM_BYTES),
        cost_estimate=cost(2),
        name="pack",
    )(core.astype(jnp.int32).reshape(1), in_vmem(where), in_hbm(tokens), in_hbm(cotangent), in_hbm(experts.T), in_hbm(probs.T))

    line_x = [along_z(own_x, d) for d in range(1, zs)]
    first_x = [along_x(own_x, c) for c in range(1, xs)]
    first_dy = [along_x(own_dy, c) for c in range(1, xs)]
    where, wgu, wd = load(where, wg, wu, wd)
    where, line_x, first_x, first_dy, own_dy = barrier((where, line_x, first_x, first_dy, own_dy))

    lead = half * 3 // 4
    lead_dy = own_dy[:lead]
    line_dy = [along_z(lead_dy, d) for d in range(1, zs)]
    rest = jnp.stack(line_x)
    more = [along_x(rest, c) for c in range(1, xs)]
    rows_x, ranks, weight, metas = [], [], [], []

    def take_tokens(where, near, far):
        outs = [((count, group, features), BF16), ((zs * count, rows), F32), ((zs * count, rows), F32),
                ((zs, 2 * kinds, rows), F32)]
        where, results = on_vmem(functools.partial(select_tokens, span), "select_tokens", 2, outs, where, (near, far))
        for held, result in zip((rows_x, ranks, weight, metas), results):
            held.append(result)
        return where

    def take_cotangents(where, c, near, far, near_tail, far_tail):
        outs = [((count, group, features), BF16)]
        return on_vmem(functools.partial(select_cotangents, c), "select_cotangents", 1, outs, where,
                       (ranks[c], near, far, near_tail, far_tail))

    near = jnp.concatenate([own_x[None], rest])
    where = take_tokens(where, near, swap(near))
    where, line_dy, more = barrier((where, line_dy, more))
    groups_x = [jnp.concatenate([a[None], b]) for a, b in zip(first_x, more)]

    rest = jnp.stack(line_dy)
    more = [along_x(rest, c) for c in range(1, xs)]
    tail = jnp.stack([own_dy[lead:]] + [block[lead:] for block in first_dy])
    tails = [along_z(tail, d) for d in range(1, zs)]
    near = [jnp.concatenate([lead_dy[None], rest])]
    far = [swap(near[0])]
    rows_dy = []
    for group_x in groups_x:
        where = take_tokens(where, group_x, swap(group_x))
    outs = [((count, hidden, slots), F32)] * 3 + [((count, hidden, slots), BF16), ((count, rows, slots), BF16)]
    where, (*factors, gated, holds) = on_vmem(functools.partial(forward_kernel, xs), "forward", 5, outs, where,
                                              (wgu, *ranks, *weight, *rows_x))
    where, more, tails = barrier((where, more, tails))
    near += [jnp.concatenate([a[None, :lead], b]) for a, b in zip(first_dy, more)]
    far += [swap(block) for block in near[1:]]
    near_tail = jnp.stack([tail] + tails)
    far_tail = swap(near_tail)
    for c in range(xs):
        where, got = take_cotangents(where, c, near[c], far[c], near_tail, far_tail)
        rows_dy += got

    outs = [((count, 2 * hidden, slots), BF16), ((count, slots, features), BF16), ((count, positions, rows), F32)]
    where, (dboth, rows_in, prob) = on_vmem(
        functools.partial(backward_kernel, xs), "backward", 6, outs, where,
        (wgu, wd, *factors, holds, *rows_dy))
    height = packed + 16 * pl.cdiv(kinds, 16)
    split = 2 * height // 3 // 16 * 16
    chip = [None] * xs
    for c in list(range(1, xs)) + [0]:
        where, (own, other) = on_vmem(
            functools.partial(put_back, span, c * zs), "put_back", 2, [((zs, height, rows), BF16)] * 2, where,
            (ranks[c], metas[c], rows_in, prob), False)
        chip[c] = own, swap(other)

    def both_cores(c, index):
        own, other = chip[c]
        return own[index].astype(F32) + other[index].astype(F32)

    def weights(where, source, number, shared, awaited):
        depth = min(count, 3)
        operands = [in_vmem(array) for array in (source, *shared)]
        *grads, where = pl.pallas_call(
            functools.partial(weights_kernel, xs, number),
            in_specs=[IN_VMEM] * (1 + len(operands)) + [pl.BlockSpec(memory_space=pl.ANY)] * len(awaited),
            out_specs=[pl.BlockSpec(memory_space=pl.ANY)] * number + [IN_VMEM],
            out_shape=[jax.ShapeDtypeStruct((count, hidden, features), BF16)] * number + [vmem_shape(WHERE, jnp.int32)],
            scratch_shapes=[pltpu.VMEM((depth, number * hidden, features), BF16), pltpu.SemaphoreType.DMA((depth, number))],
            compiler_params=pltpu.CompilerParams(vmem_limit_bytes=VMEM_BYTES),
            cost_estimate=cost(3 * number),
            name="weights",
        )(in_vmem(where), *operands, *awaited)
        return where, grads

    first, last = slice(0, split), slice(split, height)
    crossing = [both_cores(c, (slice(None), first)).astype(BF16) for c in range(1, xs)]
    sides = [jnp.stack([both_cores(c, (d, last)) for c in range(xs)]) for d in range(zs)]
    lining = [side.astype(BF16) for side in sides[1:]]
    hops = [along_x(array, -c) for c, array in enumerate(crossing, 1)]
    shifts = [along_z(array, -d) for d, array in enumerate(lining, 1)]
    where, (grad_gate, grad_up) = weights(where, dboth, 2, rows_x, crossing + lining)
    outs = [((split, rows), BF16 if d else F32) for d in range(zs)]
    outs += [((height - split, rows), BF16 if c else F32) for c in range(xs)]
    where, sums = on_vmem(functools.partial(middle_sums, zs, xs), "middle_sums", 1, outs, where,
                          (*chip[0], sides[0], *hops, *shifts), False)
    parts = [along_z(sums[d], -d) if d else sums[d] for d in range(zs)]
    parts += [along_x(sums[zs + c], -c) if c else sums[zs] for c in range(xs)]
    where, (grad_down,) = weights(where, gated, 1, rows_dy, [array for array in sums if array.dtype == BF16])
    where, (mine,) = on_vmem(functools.partial(last_sums, zs, xs), "last_sums", 1, [((height, rows), BF16)], where,
                             parts, False)
    outs = [((rows, features), BF16), ((top, rows), F32)]
    where, (grad_tokens, grad_probs) = on_vmem(unpack, "unpack", 1, outs, where, (mine, swap(mine)), False)
    grad_probs = grad_probs.T
    shape = (halves, quarter, features)
    return (
        grad_tokens,
        grad_probs,
        jnp.swapaxes(grad_gate.reshape(shape), 1, 2),
        jnp.swapaxes(grad_up.reshape(shape), 1, 2),
        grad_down.reshape(shape),
    )


def solution(mesh):
    return jax.shard_map(
        per_device,
        mesh=mesh,
        in_specs=(
            P(("groups", "expert", "blk"), None),
            P(("groups", "expert", "blk"), None),
            P(("groups", "expert", "blk"), None),
            P(("groups", "expert", "blk"), None),
            P(("expert", "blk"), None, "tensor"),
            P(("expert", "blk"), None, "tensor"),
            P(("expert", "blk"), "tensor", None),
        ),
        out_specs=(
            P(("groups", "expert", "blk"), None),
            P(("groups", "expert", "blk"), None),
            P(("groups", "expert", "blk"), None, "tensor"),
            P(("groups", "expert", "blk"), None, "tensor"),
            P(("groups", "expert", "blk"), "tensor", None),
        ),
        check_vma=False,
    )
```

```python
import functools

import jax
import jax.numpy as jnp
from jax import lax
from jax.experimental import pallas as pl
from jax.experimental.pallas import tpu as pltpu
from jax.sharding import PartitionSpec as P

MOST = 16
BF16, F32 = jnp.bfloat16, jnp.float32
LAST = (((1,), (1,)), ((), ()))
LEAD = (((0,), (0,)), ((), ()))
VMEM_BYTES = 12 * 1024 * 1024


def cost(micros):
    return pl.CostEstimate(flops=1000, bytes_accessed=int(micros * 3_000_000), transcendentals=0)


def dot(a, b, dims):
    return lax.dot_general(a, b, dims, preferred_element_type=F32)


def iota(shape, dim):
    return lax.broadcasted_iota(jnp.int32, shape, dim)


def ranks_and_probs(first, meta, span, count):
    sources, height, tokens = meta.shape
    kinds = height // 2
    wanted = ((first + span * iota((count, tokens), 0)) >> 1).astype(F32)
    named, weight = [], []
    for source in range(sources):
        entry = meta[source].astype(F32)
        hit = jnp.zeros((count, tokens), F32)
        prob = jnp.zeros((count, tokens), F32)
        for kind in range(kinds):
            same = entry[kind : kind + 1] == wanted
            hit = jnp.where(same, 1.0, hit)
            prob = jnp.where(same, entry[kinds + kind : kinds + kind + 1], prob)
        named.append(hit)
        weight.append(prob)
    named = jnp.concatenate(named)
    before = (iota((tokens, tokens), 0) < iota((tokens, tokens), 1)).astype(F32).astype(BF16)
    rank = jnp.dot(named.astype(BF16), before, preferred_element_type=F32)
    return jnp.where(named > 0, rank, -1.0), jnp.concatenate(weight)


def slot_matrix(rank):
    count, tokens = rank.shape
    wide = jnp.broadcast_to(rank[:, None, :], (count, MOST, tokens)).reshape(count * MOST, tokens)
    place = (iota((count * MOST, tokens), 0) & (MOST - 1)).astype(F32)
    return jnp.where(wide == place, 1.0, 0.0).astype(BF16)


def select(rank, near, far, rows_ref):
    count, sources = rows_ref.shape[0], rows_ref.shape[1] // MOST
    for source in range(sources):
        pick = slot_matrix(rank[source * count : (source + 1) * count])
        both = jnp.concatenate([near(source), far(source)], axis=0)
        rows = jnp.dot(pick, both, preferred_element_type=F32).astype(BF16)
        rows_ref[:, source * MOST : (source + 1) * MOST, :] = rows.reshape(count, MOST, rows.shape[1])


def unpacked(piece, half, features):
    chunks = features // piece.shape[1]
    return jnp.concatenate([piece[chunk * half : (chunk + 1) * half] for chunk in range(chunks)], axis=1)


def store_packed(ref, index, rows):
    half, features = rows.shape
    lanes = ref.shape[-1]
    for chunk in range(features // lanes):
        ref[(*index, slice(chunk * half, (chunk + 1) * half))] = rows[:, chunk * lanes : (chunk + 1) * lanes]


def pack(core_ref, where_ref, tokens_ref, cotangent_ref, experts_ref, probs_ref, x_ref, dy_ref, token_ref, half_scr, experts_scr,
         chosen_scr, ids_scr, prob_scr, sems):
    second = core_ref[0] == 1
    half = dy_ref.shape[0]
    top, kinds = experts_ref.shape[0], ids_scr.shape[0]
    mine = pl.ds(pl.multiple_of(core_ref[0] * half, half), half)
    pairs = ((tokens_ref.at[mine], half_scr), (experts_ref, experts_scr), (probs_ref, chosen_scr),
             (cotangent_ref.at[mine], dy_ref))
    copies = [pltpu.make_async_copy(source, target, sems.at[at]) for at, (source, target) in enumerate(pairs)]
    for copy in copies:
        copy.start()
    pass_on(where_ref, token_ref)
    for copy in copies:
        copy.wait()
    store_packed(x_ref, (), half_scr[...])
    ids_scr[...] = jnp.full(ids_scr.shape, -1.0, F32)
    prob_scr[...] = jnp.zeros(prob_scr.shape, F32)
    ids_scr[:top] = experts_scr[...].astype(F32)
    prob_scr[:top] = chosen_scr[...].astype(F32)
    lines = [jnp.where(second, pltpu.roll(ref[...], half, 1), ref[...]) for ref in (ids_scr, prob_scr)]
    x_ref[x_ref.shape[0] - 2 * kinds :] = jnp.concatenate(lines, axis=0).astype(BF16)


def select_tokens(span, where_ref, near_ref, far_ref, rows_ref, rank_ref, weight_ref, meta_ref):
    half, features, height = rank_ref.shape[1] // 2, rows_ref.shape[2], meta_ref.shape[1]
    meta = near_ref[:, near_ref.shape[1] - height :, :].astype(F32)
    rank, weight = ranks_and_probs(where_ref[0:1, : meta.shape[2]], meta, span, rows_ref.shape[0])
    rank_ref[...] = rank
    weight_ref[...] = weight
    meta_ref[...] = meta
    select(rank, lambda source: unpacked(near_ref[source], half, features),
           lambda source: unpacked(far_ref[source], half, features), rows_ref)


def select_cotangents(c, where_ref, rank_ref, near_ref, far_ref, near_tail, far_tail, rows_ref):
    whole = lambda first, tail: lambda source: jnp.concatenate([first[source], tail[source, c]], axis=0)
    select(rank_ref[...], whole(near_ref, near_tail), whole(far_ref, far_tail), rows_ref)


def joined(refs, index):
    return jnp.concatenate([ref[index] for ref in refs], axis=0)


def each(count, body):
    def step(index, carry):
        body(index)
        return carry

    lax.fori_loop(0, count, step, 0, unroll=8 if count % 8 == 0 else 1)


def forward_kernel(groups, where_ref, both_ref, *refs):
    rank_refs, weight_refs, rows_refs = refs[:groups], refs[groups : 2 * groups], refs[2 * groups : 3 * groups]
    hidden_ref, fgate_ref, fup_ref, gated_ref, holds_ref = refs[3 * groups :]
    count, tokens, slots = holds_ref.shape
    rank = joined(rank_refs, ...).astype(BF16)
    weight = joined(weight_refs, ...).astype(BF16)
    place = (iota((tokens, slots), 1) & (MOST - 1)).astype(F32)
    row, lane = iota((rank.shape[0], slots), 0), iota((rank.shape[0], slots), 1)

    def body(expert):
        spread = jnp.where(row == (lane // MOST) * count + expert, 1.0, 0.0).astype(BF16)
        holds = dot(rank, spread, LEAD) == place
        scale = jnp.sum(jnp.where(holds, dot(weight, spread, LEAD), 0.0), axis=0, keepdims=True)
        holds_ref[expert] = jnp.where(holds, 1.0, 0.0).astype(BF16)
        rows = joined(rows_refs, expert)
        both = dot(both_ref[expert], rows, LAST)
        gate, up = both[: both.shape[0] // 2], both[both.shape[0] // 2 :]
        sigmoid = 1.0 / (1.0 + jnp.exp(-gate))
        active = gate * sigmoid
        hidden = active * up
        hidden_ref[expert] = hidden
        gated_ref[expert] = (scale * hidden).astype(BF16)
        fgate_ref[expert] = scale * up * sigmoid * (1.0 + gate * (1.0 - sigmoid))
        fup_ref[expert] = scale * active

    each(count, body)


def backward_kernel(groups, where_ref, both_ref, wd_ref, hidden_ref, fgate_ref, fup_ref, holds_ref, *refs):
    rows_refs, (dboth_ref, input_ref, prob_ref) = refs[:groups], refs[groups:]
    count, slots, _ = input_ref.shape
    sources = prob_ref.shape[1]
    block = jnp.where(iota((sources, slots), 0) == iota((sources, slots), 1) // MOST, 1.0, 0.0).astype(BF16)

    def body(expert):
        raw = dot(wd_ref[expert], joined(rows_refs, expert), LAST)
        dgate = (raw * fgate_ref[expert]).astype(BF16)
        dup = (raw * fup_ref[expert]).astype(BF16)
        dboth = jnp.concatenate([dgate, dup], axis=0)
        dboth_ref[expert] = dboth
        input_ref[expert] = dot(dboth, both_ref[expert], LEAD).astype(BF16)
        prob = jnp.sum(hidden_ref[expert] * raw, axis=0, keepdims=True)
        prob_ref[expert] = dot(block, (holds_ref[expert].astype(F32) * prob).astype(BF16), LAST)

    each(count, body)


def put_back(span, base, where_ref, rank_ref, meta_ref, input_ref, prob_ref, own_ref, other_ref):
    count, _, features = input_ref.shape
    tokens = rank_ref.shape[1]
    half, kinds = tokens // 2, meta_ref.shape[1] // 2
    tail = own_ref.shape[1] - features // own_ref.shape[2] * half
    wanted = ((where_ref[0:1, :tokens] + span * iota((count, tokens), 0)) >> 1).astype(F32)
    for source in range(own_ref.shape[0]):
        number = base + source
        pick = slot_matrix(rank_ref[source * count : (source + 1) * count])
        rows = input_ref[:, number * MOST : (number + 1) * MOST, :].reshape(count * MOST, features)
        part = dot(pick, rows, LEAD).astype(BF16)
        store_packed(own_ref, (source,), part[:half])
        store_packed(other_ref, (source,), part[half:])
        prob = prob_ref[:, number, :]
        entry = meta_ref[source]
        lines = jnp.zeros((tail, tokens), F32)
        for kind in range(kinds):
            line = jnp.sum(jnp.where(entry[kind : kind + 1] == wanted, prob, 0.0), axis=0, keepdims=True)
            lines = jnp.where(iota((tail, tokens), 0) == kind, line, lines)
        own_ref[source, own_ref.shape[1] - tail :] = lines.astype(BF16)
        other_ref[source, own_ref.shape[1] - tail :] = pltpu.roll(lines, half, 1).astype(BF16)


def weights_kernel(groups, number, where_ref, hidden_ref, *refs):
    rows_refs = refs[:groups]
    targets, token_ref, slots_ref, sems = refs[-3 - number : -3], *refs[-3:]
    count, depth, height = hidden_ref.shape[0], slots_ref.shape[0], hidden_ref.shape[1] // number

    def copies(expert):
        slot = lax.rem(expert, depth)
        return [
            pltpu.make_async_copy(slots_ref.at[slot, pl.ds(at * height, height)], target.at[expert], sems.at[slot, at])
            for at, target in enumerate(targets)
        ]

    def body(expert, carry):
        @pl.when(expert >= depth)
        def _():
            for copy in copies(expert - depth):
                copy.wait()

        grads = jnp.dot(hidden_ref[expert], joined(rows_refs, expert), preferred_element_type=F32)
        slots_ref[lax.rem(expert, depth)] = grads.astype(BF16)
        for copy in copies(expert):
            copy.start()
        return carry

    lax.fori_loop(0, count, body, 0)
    for expert in range(max(count - depth, 0), count):
        for copy in copies(expert):
            copy.wait()
    pass_on(where_ref, token_ref)


def middle_sums(zs, xs, where_ref, own_ref, other_ref, base_ref, *refs):
    hops, shifts, outs = refs[: xs - 1], refs[xs - 1 : xs + zs - 2], refs[xs + zs - 2 :]
    size = hops[0].shape[1]
    for place in range(zs):
        total = own_ref[place, :size].astype(F32) + other_ref[place, :size].astype(F32)
        for hop in hops:
            total = total + hop[place].astype(F32)
        outs[place][...] = total.astype(outs[place].dtype)
    for place in range(xs):
        total = base_ref[place]
        for piece in shifts:
            total = total + piece[place].astype(F32)
        outs[zs + place][...] = total.astype(outs[zs + place].dtype)


def last_sums(zs, xs, where_ref, *refs):
    first, last, out = refs[:zs], refs[zs : zs + xs], refs[-1]
    size = first[0].shape[0]
    for refs, rows in ((first, slice(0, size)), (last, slice(size, out.shape[0]))):
        total = refs[0][...]
        for ref in refs[1:]:
            total = total + ref[...].astype(F32)
        out[rows] = total.astype(BF16)


def unpack(where_ref, mine_ref, theirs_ref, tokens_ref, probs_ref):
    mine, theirs = mine_ref[...].astype(F32), theirs_ref[...].astype(F32)
    second = jnp.broadcast_to(where_ref[1:2, : mine.shape[1]], mine.shape) == 1
    half, features = tokens_ref.shape[0] // 2, tokens_ref.shape[1]
    low, high = jnp.where(second, theirs, mine), jnp.where(second, mine, theirs)
    tokens_ref[:half] = unpacked(low, half, features).astype(BF16)
    tokens_ref[half:] = unpacked(high, half, features).astype(BF16)
    at = features // low.shape[1] * half
    low, high = low[at:], high[at:]
    both = jnp.where(iota(low.shape, 1) < half, low, pltpu.roll(high, half, 1))
    probs_ref[...] = both[: probs_ref.shape[0]]


def in_vmem(array):
    return pltpu.with_memory_space_constraint(array, pltpu.VMEM)


def in_hbm(array):
    return pltpu.with_memory_space_constraint(array, pltpu.HBM)


def vmem_shape(shape, dtype):
    return pltpu.VMEM(shape, dtype)


def in_hbm(array):
    return pltpu.with_memory_space_constraint(array, pltpu.HBM)


def vmem_shape(shape, dtype):
    return pltpu.VMEM(shape, dtype)


def pass_on(where_ref, token_ref):
    token_ref[...] = where_ref[...]


def load_kernel(where_ref, gate_ref, up_ref, down_ref, both_ref, down_held, token_ref, sems):
    hidden = gate_ref.shape[1]
    pairs = ((gate_ref, both_ref.at[:, :hidden]), (up_ref, both_ref.at[:, hidden:]), (down_ref, down_held))
    copies = [pltpu.make_async_copy(source, target, sems.at[at]) for at, (source, target) in enumerate(pairs)]
    for copy in copies:
        copy.start()
    pass_on(where_ref, token_ref)
    for copy in copies:
        copy.wait()


SCALARS = pl.BlockSpec(memory_space=pltpu.SMEM)
IN_VMEM = pl.BlockSpec(memory_space=pltpu.VMEM)
WHERE = (8, 128)


def load(where, gate, up, down):
    count, hidden, features = gate.shape
    both, down, where = pl.pallas_call(
        load_kernel,
        in_specs=[IN_VMEM] + [pl.BlockSpec(memory_space=pl.ANY)] * 3,
        out_specs=[IN_VMEM] * 3,
        out_shape=[vmem_shape((count, 2 * hidden, features), gate.dtype), vmem_shape(down.shape, down.dtype),
                   vmem_shape(WHERE, jnp.int32)],
        scratch_shapes=[pltpu.SemaphoreType.DMA((3,))],
        compiler_params=pltpu.CompilerParams(vmem_limit_bytes=VMEM_BYTES),
        cost_estimate=cost(7),
        name="load",
    )(in_vmem(where), in_hbm(gate), in_hbm(up), in_hbm(down))
    return where, both, down


def on_vmem(kernel, name, micros, outs, where, operands, stay=True, scratch=()):
    def body(where_ref, *refs):
        at = len(operands) + len(outs)
        kernel(where_ref, *refs[:at], *refs[at + 1 :])
        pass_on(where_ref, refs[at])

    *held, where = pl.pallas_call(
        body,
        in_specs=[IN_VMEM] * (1 + len(operands)),
        out_specs=[IN_VMEM] * (len(outs) + 1),
        out_shape=[(vmem_shape if stay else jax.ShapeDtypeStruct)(shape, dtype) for shape, dtype in outs] + [vmem_shape(WHERE, jnp.int32)],
        scratch_shapes=list(scratch),
        compiler_params=pltpu.CompilerParams(vmem_limit_bytes=VMEM_BYTES),
        cost_estimate=cost(micros),
        name=name,
    )(in_vmem(where), *map(in_vmem, operands))
    return where, held


def per_device(tokens, cotangent, probs, experts, w_gate, w_up, w_down):
    rows, features = tokens.shape
    top = experts.shape[1]
    zs, xs = lax.axis_size("expert"), lax.axis_size("blk")
    cores = lax.axis_size("tensor")
    positions = zs * xs
    half = rows // cores
    halves, _, quarter = w_gate.shape
    span = 2 if halves % 2 == 0 else 1
    count = halves // span
    hidden = span * quarter
    slots = positions * MOST
    core = lax.axis_index("tensor")
    position = lax.axis_index("expert") * xs + lax.axis_index("blk")
    kinds = 8 * pl.cdiv(top, 8)
    barrier = lax.optimization_barrier

    def swap(array):
        return lax.ppermute(array, "tensor", [(i, (i + 1) % cores) for i in range(cores)])

    def along_z(array, by):
        return lax.ppermute(array, "expert", [(i, (i + by) % zs) for i in range(zs)])

    def along_x(array, by):
        return lax.ppermute(array, "blk", [(i, (i + by) % xs) for i in range(xs)])

    wg = jnp.swapaxes(w_gate, 1, 2).reshape(count, hidden, features)
    wu = jnp.swapaxes(w_up, 1, 2).reshape(count, hidden, features)
    wd = w_down.reshape(count, hidden, features)
    where = jnp.where(iota(WHERE, 0) == 0, position * halves, core).astype(jnp.int32)
    group = zs * MOST
    packed = features // rows * half
    own_x, own_dy, where = pl.pallas_call(
        pack,
        in_specs=[SCALARS, IN_VMEM] + [pl.BlockSpec(memory_space=pl.ANY)] * 4,
        out_specs=[IN_VMEM] * 3,
        out_shape=[jax.ShapeDtypeStruct((packed + 2 * kinds, rows), BF16), jax.ShapeDtypeStruct((half, features), BF16),
                   vmem_shape(WHERE, jnp.int32)],
        scratch_shapes=[pltpu.VMEM((half, features), BF16), pltpu.VMEM((top, rows), jnp.int32),
                        pltpu.VMEM((top, rows), BF16), pltpu.VMEM((kinds, rows), F32), pltpu.VMEM((kinds, rows), F32),
                        pltpu.SemaphoreType.DMA((4,))],
        compiler_params=pltpu.CompilerParams(vmem_limit_bytes=VMEM_BYTES),
        cost_estimate=cost(2),
        name="pack",
    )(core.astype(jnp.int32).reshape(1), in_vmem(where), in_hbm(tokens), in_hbm(cotangent), in_hbm(experts.T), in_hbm(probs.T))

    line_x = [along_z(own_x, d) for d in range(1, zs)]
    first_x = [along_x(own_x, c) for c in range(1, xs)]
    first_dy = [along_x(own_dy, c) for c in range(1, xs)]
    where, wgu, wd = load(where, wg, wu, wd)
    where, line_x, first_x, first_dy, own_dy = barrier((where, line_x, first_x, first_dy, own_dy))

    lead = half * 3 // 4
    lead_dy = own_dy[:lead]
    line_dy = [along_z(lead_dy, d) for d in range(1, zs)]
    rest = jnp.stack(line_x)
    more = [along_x(rest, c) for c in range(1, xs)]
    rows_x, ranks, weight, metas = [], [], [], []

    def take_tokens(where, near, far):
        outs = [((count, group, features), BF16), ((zs * count, rows), F32), ((zs * count, rows), F32),
                ((zs, 2 * kinds, rows), F32)]
        where, results = on_vmem(functools.partial(select_tokens, span), "select_tokens", 2, outs, where, (near, far))
        for held, result in zip((rows_x, ranks, weight, metas), results):
            held.append(result)
        return where

    def take_cotangents(where, c, near, far, near_tail, far_tail):
        outs = [((count, group, features), BF16)]
        return on_vmem(functools.partial(select_cotangents, c), "select_cotangents", 1, outs, where,
                       (ranks[c], near, far, near_tail, far_tail))

    near = jnp.concatenate([own_x[None], rest])
    where = take_tokens(where, near, swap(near))
    where, line_dy, more = barrier((where, line_dy, more))
    groups_x = [jnp.concatenate([a[None], b]) for a, b in zip(first_x, more)]

    rest = jnp.stack(line_dy)
    more = [along_x(rest, c) for c in range(1, xs)]
    tail = jnp.stack([own_dy[lead:]] + [block[lead:] for block in first_dy])
    tails = [along_z(tail, d) for d in range(1, zs)]
    near = [jnp.concatenate([lead_dy[None], rest])]
    far = [swap(near[0])]
    rows_dy = []
    for group_x in groups_x:
        where = take_tokens(where, group_x, swap(group_x))
    outs = [((count, hidden, slots), F32)] * 3 + [((count, hidden, slots), BF16), ((count, rows, slots), BF16)]
    where, (*factors, gated, holds) = on_vmem(functools.partial(forward_kernel, xs), "forward", 5, outs, where,
                                              (wgu, *ranks, *weight, *rows_x))
    where, more, tails = barrier((where, more, tails))
    near += [jnp.concatenate([a[None, :lead], b]) for a, b in zip(first_dy, more)]
    far += [swap(block) for block in near[1:]]
    near_tail = jnp.stack([tail] + tails)
    far_tail = swap(near_tail)
    for c in range(xs):
        where, got = take_cotangents(where, c, near[c], far[c], near_tail, far_tail)
        rows_dy += got

    outs = [((count, 2 * hidden, slots), BF16), ((count, slots, features), BF16), ((count, positions, rows), F32)]
    where, (dboth, rows_in, prob) = on_vmem(
        functools.partial(backward_kernel, xs), "backward", 6, outs, where,
        (wgu, wd, *factors, holds, *rows_dy))
    height = packed + 16 * pl.cdiv(kinds, 16)
    split = 7 * height // 10 // 16 * 16
    chip = [None] * xs
    for c in list(range(1, xs)) + [0]:
        where, (own, other) = on_vmem(
            functools.partial(put_back, span, c * zs), "put_back", 2, [((zs, height, rows), BF16)] * 2, where,
            (ranks[c], metas[c], rows_in, prob), False)
        chip[c] = own, swap(other)

    def both_cores(c, index):
        own, other = chip[c]
        return own[index].astype(F32) + other[index].astype(F32)

    def weights(where, source, number, shared, awaited):
        depth = min(count, 3)
        operands = [in_vmem(array) for array in (source, *shared)]
        *grads, where = pl.pallas_call(
            functools.partial(weights_kernel, xs, number),
            in_specs=[IN_VMEM] * (1 + len(operands)) + [pl.BlockSpec(memory_space=pl.ANY)] * len(awaited),
            out_specs=[pl.BlockSpec(memory_space=pl.ANY)] * number + [IN_VMEM],
            out_shape=[jax.ShapeDtypeStruct((count, hidden, features), BF16)] * number + [vmem_shape(WHERE, jnp.int32)],
            scratch_shapes=[pltpu.VMEM((depth, number * hidden, features), BF16), pltpu.SemaphoreType.DMA((depth, number))],
            compiler_params=pltpu.CompilerParams(vmem_limit_bytes=VMEM_BYTES),
            cost_estimate=cost(3 * number),
            name="weights",
        )(in_vmem(where), *operands, *awaited)
        return where, grads

    first, last = slice(0, split), slice(split, height)
    crossing = [both_cores(c, (slice(None), first)).astype(BF16) for c in range(1, xs)]
    sides = [jnp.stack([both_cores(c, (d, last)) for c in range(xs)]) for d in range(zs)]
    lining = [side.astype(BF16) for side in sides[1:]]
    hops = [along_x(array, -c) for c, array in enumerate(crossing, 1)]
    shifts = [along_z(array, -d) for d, array in enumerate(lining, 1)]
    where, (grad_gate, grad_up) = weights(where, dboth, 2, rows_x, crossing + lining)
    outs = [((split, rows), BF16 if d else F32) for d in range(zs)]
    outs += [((height - split, rows), BF16 if c else F32) for c in range(xs)]
    where, sums = on_vmem(functools.partial(middle_sums, zs, xs), "middle_sums", 1, outs, where,
                          (*chip[0], sides[0], *hops, *shifts), False)
    parts = [along_z(sums[d], -d) if d else sums[d] for d in range(zs)]
    parts += [along_x(sums[zs + c], -c) if c else sums[zs] for c in range(xs)]
    where, (grad_down,) = weights(where, gated, 1, rows_dy, [array for array in sums if array.dtype == BF16])
    where, (mine,) = on_vmem(functools.partial(last_sums, zs, xs), "last_sums", 1, [((height, rows), BF16)], where,
                             parts, False)
    outs = [((rows, features), BF16), ((top, rows), F32)]
    where, (grad_tokens, grad_probs) = on_vmem(unpack, "unpack", 1, outs, where, (mine, swap(mine)), False)
    grad_probs = grad_probs.T
    shape = (halves, quarter, features)
    return (
        grad_tokens,
        grad_probs,
        jnp.swapaxes(grad_gate.reshape(shape), 1, 2),
        jnp.swapaxes(grad_up.reshape(shape), 1, 2),
        grad_down.reshape(shape),
    )


def solution(mesh):
    return jax.shard_map(
        per_device,
        mesh=mesh,
        in_specs=(
            P(("groups", "expert", "blk"), None),
            P(("groups", "expert", "blk"), None),
            P(("groups", "expert", "blk"), None),
            P(("groups", "expert", "blk"), None),
            P(("expert", "blk"), None, "tensor"),
            P(("expert", "blk"), None, "tensor"),
            P(("expert", "blk"), "tensor", None),
        ),
        out_specs=(
            P(("groups", "expert", "blk"), None),
            P(("groups", "expert", "blk"), None),
            P(("groups", "expert", "blk"), None, "tensor"),
            P(("groups", "expert", "blk"), None, "tensor"),
            P(("groups", "expert", "blk"), "tensor", None),
        ),
        check_vma=False,
    )
```
